32 devices in a mesh: seq: 8 (over z, y), chan: 4 (over x, core).
Axes of the slice: x: 2, y: 2, z: 4, core: 2. Of those that a mesh axis runs over, the one named last changes fastest.
Arguments:
- query_gate: float32 [16, 65536], P('chan', 'seq'), may hold values from -6 to 6
- key_gate: float32 [16, 65536], P('chan', 'seq'), may hold values from -6 to 6
- value_input: float32 [16, 65536], P('chan', 'seq'), may hold values from -6 to 6
- filter_taps: float32 [4, 65536], P(None, ('seq', 'chan')), may hold values from -2 to 2
- cotangent: float32 [16, 65536], P('chan', 'seq'), may hold values from -6 to 6
Outputs:
- query_grad: float32 [16, 65536], P('chan', 'seq')
- key_grad: float32 [16, 65536], P('chan', 'seq')
- value_grad: float32 [16, 65536], P('chan', 'seq')
The draws below stay inside these ranges and needn't reach their ends.
All inputs are finite; a program needn't handle non-finite values.
Results may differ from the reference program's by a relative error of at most 0.00013.
Values sent between devices are 32-bit elements; how exact they have to be, the bound alone decides.
A program may use at most 64 MiB of HBM per device.

```python
import math
import jax
import jax.numpy as jnp
from jax import lax

FILTERS = 4
CHANNELS = 16
LENGTH = 65536


def draw_filter_taps(key, part):
    noise_seed, rate_seed = jax.random.split(key)
    lag_index = jnp.arange(LENGTH, dtype=jnp.float32)[None, :]
    decay_span = jnp.exp(jax.random.uniform(rate_seed, (FILTERS, 1), jnp.float32, math.log(4.0), math.log(64.0)))
    noise_draw = jnp.clip(jax.random.normal(noise_seed, (FILTERS, LENGTH), jnp.float32), -6.0, 6.0)
    far_level = 1.2 / math.sqrt(LENGTH)
    return noise_draw * (0.3 * jnp.exp(-lag_index / decay_span) + far_level)


def shard_levels(key, extent, shards, smallest, top_value):
    def one(position, blocks):
        draws = jax.random.uniform(jax.random.fold_in(jax.random.fold_in(key, 6), position), (blocks,), jnp.float32, smallest / len(shards), top_value / len(shards))
        return jnp.repeat(jnp.exp(draws), extent[position] // blocks).reshape((-1,) + (1,) * (len(extent) - position - 1))

    level = one(*shards[0])
    for cut in shards[1:]:
        level = level * one(*cut)
    return level


def gaussian(key, shape, width, reach, cuts=(), kind=jnp.bfloat16):
    entries = width * jax.random.normal(key, shape, jnp.float32)
    if cuts:
        entries = entries * shard_levels(key, shape, cuts, -0.22, 0.18)
    return jnp.clip(entries, -reach, reach).astype(kind)


def setup_inputs(seed: int = 0) -> dict:
    splits = jax.random.split(jax.random.key(seed), 6)
    query_gate = gaussian(splits[0], (CHANNELS, LENGTH), 1.0, 6.0, ((0, 4), (1, 8)), jnp.float32)
    key_gate = gaussian(splits[1], (CHANNELS, LENGTH), 1.0, 6.0, ((0, 4), (1, 8)), jnp.float32)
    value_input = gaussian(splits[2], (CHANNELS, LENGTH), 1.0, 6.0, ((0, 4), (1, 8)), jnp.float32)
    filter_taps = draw_filter_taps(jax.random.fold_in(splits[5], 71), 0)
    cotangent = gaussian(splits[4], (CHANNELS, LENGTH), 1.0, 6.0, ((0, 4), (1, 8)), jnp.float32)
    return {"query_gate": query_gate, "key_gate": key_gate, "value_input": value_input, "filter_taps": filter_taps, "cotangent": cotangent}


def reference(query_gate, key_gate, value_input, filter_taps, cotangent):
    period = 2 * LENGTH
    spectra = jnp.fft.rfft(filter_taps, n=period, axis=-1)
    groups = CHANNELS // FILTERS

    def one_group(items):
        query_rows, key_rows, value_rows, grad_rows = items
        gated = key_rows * value_rows
        convolved = jnp.fft.irfft(jnp.fft.rfft(gated, n=period, axis=-1) * spectra, n=period, axis=-1)[:, :LENGTH]
        weighted = grad_rows * query_rows
        gated_grad = jnp.fft.irfft(jnp.fft.rfft(weighted, n=period, axis=-1) * jnp.conj(spectra), n=period, axis=-1)[:, :LENGTH]
        convolved = convolved.astype(jnp.float32)
        gated_grad = gated_grad.astype(jnp.float32)
        return grad_rows * convolved, gated_grad * value_rows, gated_grad * key_rows

    shaped = tuple(array.reshape(groups, FILTERS, LENGTH) for array in (query_gate, key_gate, value_input, cotangent))
    query_grad, key_grad, value_grad = lax.map(one_group, shaped)
    return (query_grad.reshape(CHANNELS, LENGTH), key_grad.reshape(CHANNELS, LENGTH), value_grad.reshape(CHANNELS, LENGTH))
```

```python
from functools import partial
import math

import jax
import jax.numpy as jnp
import ml_dtypes
import numpy as np
from jax import lax
from jax.experimental import pallas as pl
from jax.experimental.pallas import tpu as pltpu
from jax.sharding import PartitionSpec as P

MESH = pl.DeviceIdType.MESH
SIDE = 256
LANES = 128


def halves(table):
    high = table.astype(ml_dtypes.bfloat16)
    low = (table - high.astype(np.float64)).astype(ml_dtypes.bfloat16)
    return (high, low)


def fourier_tables():
    total = SIDE * SIDE
    index = np.arange(SIDE, dtype=np.float64)
    outer = 2.0 * np.pi * np.outer(index + 0.25, index) / SIDE
    first = np.concatenate([np.cos(outer), -np.sin(outer)], axis=0)
    last = first.T / total
    inner = 2.0 * np.pi * (np.outer(index, index) % SIDE) / SIDE
    cosine, sine = np.cos(inner), np.sin(inner)
    middle = np.block([[cosine, -sine], [sine, cosine]])
    back = middle.T
    twist = 2.0 * np.pi * np.outer(index + 0.25, index) / total
    return (
        *halves(first),
        *halves(middle),
        *halves(back),
        *halves(last),
        np.cos(twist).astype(np.float32),
        (-np.sin(twist)).astype(np.float32),
    )


def split(value):
    high = value.astype(jnp.bfloat16)
    low = (value - high.astype(jnp.float32)).astype(jnp.bfloat16)
    return high, low


def mul(left, right):
    dot = partial(jnp.dot, preferred_element_type=jnp.float32)
    return dot(left[0], right[0]) + (dot(left[0], right[1]) + dot(left[1], right[0]))


def row_kernel(
    blocks, groups, k_ref, v_ref, q_ref, c_ref, taps_ref,
    t0, t1, t2, t3, t4, t5, t6, t7, t8, t9, out_ref,
    pieces, tap_pieces, rows, filt, result, back,
    first_hi, first_lo, mid_hi, mid_lo, inv_hi, inv_lo, last_hi, last_lo, twist_re, twist_im,
    table_sem, tap_send, tap_recv, slab_send, slab_recv, in_send, in_recv, out_send, out_recv,
):
    me = lax.axis_index("seq")
    col = lax.axis_index("chan")
    count = k_ref.shape[0]

    held = (first_hi, first_lo, mid_hi, mid_lo, inv_hi, inv_lo, last_hi, last_lo, twist_re, twist_im)
    loads = [
        pltpu.make_async_copy(source, target, table_sem.at[place])
        for place, (source, target) in enumerate(zip((t0, t1, t2, t3, t4, t5, t6, t7, t8, t9), held))
    ]
    for load in loads:
        load.start()

    barrier = pltpu.get_barrier_semaphore()
    for step in range(1, blocks):
        pl.semaphore_signal(barrier, inc=1, device_id=(lax.rem(me + step, blocks), col), device_id_type=MESH)
    for step in range(1, groups):
        pl.semaphore_signal(barrier, inc=1, device_id=(me, lax.rem(col + step, groups)), device_id_type=MESH)

    for row in range(taps_ref.shape[1] // SIDE):
        for half in range(SIDE // LANES):
            tokens = slice(row * SIDE + half * LANES, row * SIDE + (half + 1) * LANES)
            lanes = slice(half * LANES, (half + 1) * LANES)
            tap_pieces[:, row, lanes] = taps_ref[:, tokens]
    for row in range(k_ref.shape[1] // SIDE):
        for half in range(SIDE // LANES):
            tokens = slice(row * SIDE + half * LANES, row * SIDE + (half + 1) * LANES)
            lanes = slice(half * LANES, (half + 1) * LANES)
            pieces[:count, row, lanes] = k_ref[:, tokens] * v_ref[:, tokens]
            pieces[count:, row, lanes] = c_ref[:, tokens] * q_ref[:, tokens]

    pl.semaphore_wait(barrier, blocks + groups - 2)

    tap_copies, in_copies = [], []
    for step in range(1, blocks):
        target = lax.rem(me + step, blocks)
        copy = pltpu.make_async_remote_copy(
            src_ref=tap_pieces.at[lax.rem(target, count)], dst_ref=filt.at[me, col],
            send_sem=tap_send.at[step], recv_sem=tap_recv.at[step],
            device_id=(target, col), device_id_type=MESH,
        )
        copy.start()
        tap_copies.append(copy)
    for step in range(1, blocks):
        target = lax.rem(me + step, blocks)
        copy = pltpu.make_async_remote_copy(
            src_ref=pieces.at[target], dst_ref=rows.at[me],
            send_sem=in_send.at[step], recv_sem=in_recv.at[step],
            device_id=(target, col), device_id_type=MESH,
        )
        copy.start()
        in_copies.append(copy)
    filt[me, col] = tap_pieces[lax.rem(me, count)]
    rows[me] = pieces[me]

    for copy in tap_copies:
        copy.wait_recv()
    slab_copies = []
    for step in range(1, groups):
        copy = pltpu.make_async_remote_copy(
            src_ref=filt.at[:, col], dst_ref=filt.at[:, col],
            send_sem=slab_send.at[step], recv_sem=slab_recv.at[step],
            device_id=(me, lax.rem(col + step, groups)), device_id_type=MESH,
        )
        copy.start()
        slab_copies.append(copy)

    for load in loads:
        load.wait()

    def spectrum(signal):
        mixed = mul((first_hi[...], first_lo[...]), split(signal))
        real, imag = mixed[:SIDE], mixed[SIDE:]
        turn_re, turn_im = twist_re[...], twist_im[...]
        twisted = jnp.concatenate(
            [real * turn_re - imag * turn_im, real * turn_im + imag * turn_re], axis=1
        )
        fine = mul(split(twisted), (mid_hi[...], mid_lo[...]))
        return fine[:, :SIDE], fine[:, SIDE:]

    for copy in in_copies:
        copy.wait_recv()
    row_re, row_im = spectrum(rows[...].reshape(SIDE, SIDE))
    for copy in slab_copies:
        copy.wait_recv()
    tap_re, tap_im = spectrum(filt[...].reshape(SIDE, SIDE))
    tap_im = tap_im * jnp.where(me < count, 1.0, -1.0)
    joined = jnp.concatenate(
        [row_re * tap_re - row_im * tap_im, row_re * tap_im + row_im * tap_re], axis=1
    )
    coarse = mul(split(joined), (inv_hi[...], inv_lo[...]))
    real, imag = coarse[:, :SIDE], coarse[:, SIDE:]
    turn_re, turn_im = twist_re[...], twist_im[...]
    level = jnp.concatenate(
        [real * turn_re + imag * turn_im, imag * turn_re - real * turn_im], axis=0
    )
    rebuilt = mul((last_hi[...], last_lo[...]), split(level))
    result[...] = rebuilt.reshape(result.shape)

    out_copies = []
    for step in range(1, blocks):
        target = lax.rem(me + step, blocks)
        copy = pltpu.make_async_remote_copy(
            src_ref=result.at[target], dst_ref=back.at[me],
            send_sem=out_send.at[step], recv_sem=out_recv.at[step],
            device_id=(target, col), device_id_type=MESH,
        )
        copy.start()
        out_copies.append(copy)
    back[me] = result[me]
    for copy in out_copies:
        copy.wait_recv()
    for row in range(back.shape[1]):
        for half in range(SIDE // LANES):
            tokens = slice(row * SIDE + half * LANES, row * SIDE + (half + 1) * LANES)
            lanes = slice(half * LANES, (half + 1) * LANES)
            out_ref[:, tokens] = back[:, row, lanes]
    for copy in tap_copies + in_copies + slab_copies + out_copies:
        copy.wait_send()


def rows_on_device(query_gate, key_gate, value_input, filter_taps, cotangent):
    count, width = query_gate.shape
    blocks = lax.axis_size("seq")
    groups = lax.axis_size("chan")
    high = width // SIDE
    tables = fourier_tables()
    f32, bf16 = jnp.float32, jnp.bfloat16
    any_space = pl.BlockSpec(memory_space=pl.ANY)
    vmem = pl.BlockSpec(memory_space=pltpu.VMEM)
    sums = pl.pallas_call(
        partial(row_kernel, blocks, groups),
        out_shape=jax.ShapeDtypeStruct((blocks, width), f32),
        in_specs=[vmem] * 5 + [any_space] * len(tables),
        out_specs=vmem,
        scratch_shapes=[
            pltpu.VMEM((blocks, high, SIDE), f32),
            pltpu.VMEM((count, high // groups, SIDE), f32),
            pltpu.VMEM((blocks, high, SIDE), f32),
            pltpu.VMEM((blocks, groups, high // groups, SIDE), f32),
            pltpu.VMEM((blocks, high, SIDE), f32),
            pltpu.VMEM((blocks, high, SIDE), f32),
            *[pltpu.VMEM(table.shape, bf16 if place < 8 else f32) for place, table in enumerate(tables)],
            pltpu.SemaphoreType.DMA((len(tables),)),
            pltpu.SemaphoreType.DMA((blocks,)),
            pltpu.SemaphoreType.DMA((blocks,)),
            pltpu.SemaphoreType.DMA((groups,)),
            pltpu.SemaphoreType.DMA((groups,)),
            pltpu.SemaphoreType.DMA((blocks,)),
            pltpu.SemaphoreType.DMA((blocks,)),
            pltpu.SemaphoreType.DMA((blocks,)),
            pltpu.SemaphoreType.DMA((blocks,)),
        ],
        compiler_params=pltpu.CompilerParams(
            collective_id=0, has_side_effects=True, vmem_limit_bytes=32 * 1024 * 1024
        ),
    )(key_gate, value_input, query_gate, cotangent, filter_taps, *[jnp.asarray(table) for table in tables])
    convolved, gated_grad = sums[:count], sums[count:]
    return (cotangent * convolved, gated_grad * value_input, gated_grad * key_gate)


def one_row_each(query_gate, filter_taps):
    count, width = query_gate.shape
    blocks = lax.axis_size("seq")
    groups = lax.axis_size("chan")
    return (
        blocks == 2 * count
        and filter_taps.shape[0] == count
        and blocks * width == SIDE * SIDE
        and width % (8 * groups * SIDE) == 0
    )


def phase_table(row_count, column_count, offset, period, direction):
    row_index = lax.broadcasted_iota(jnp.int32, (row_count, column_count), 0)
    column_index = lax.broadcasted_iota(jnp.int32, (row_count, column_count), 1)
    phases = row_index * (column_index + offset) % period
    angles = phases.astype(jnp.float32) * (direction * 2.0 * math.pi / period)
    return (jnp.cos(angles), jnp.sin(angles))


def complex_mix(formula, table_real, table_imag, data_real, data_imag):
    product = partial(jnp.einsum, formula, precision=lax.Precision.HIGHEST)
    return (
        product(table_real, data_real) - product(table_imag, data_imag),
        product(table_real, data_imag) + product(table_imag, data_real),
    )


def regroup_tokens(signal):
    return lax.all_to_all(signal, "seq", split_axis=1, concat_axis=1, tiled=True)


def regroup_spectrum(part_real, part_imag):
    return (
        lax.all_to_all(part_real, "seq", split_axis=1, concat_axis=1, tiled=True),
        lax.all_to_all(part_imag, "seq", split_axis=1, concat_axis=1, tiled=True),
    )


def finish_forward(moved_real, moved_imag, blocks, width, tokens):
    outer_real, outer_imag = phase_table(blocks, blocks, 0, blocks, -1.0)
    coarse_real, coarse_imag = complex_mix(
        "ur,crjq->cujq", outer_real, outer_imag, moved_real, moved_imag
    )
    shift_real, shift_imag = phase_table(blocks, width, 0, tokens, -1.0)
    shift_real = shift_real[None, :, None, :]
    shift_imag = shift_imag[None, :, None, :]
    twisted_real = coarse_real * shift_real - coarse_imag * shift_imag
    twisted_imag = coarse_real * shift_imag + coarse_imag * shift_real
    inner_real, inner_imag = phase_table(width, width, 0, width, -1.0)
    return complex_mix("qv,cujq->cujv", inner_real, inner_imag, twisted_real, twisted_imag)


def start_inverse(spectrum_real, spectrum_imag, blocks, width, tokens):
    inner_real, inner_imag = phase_table(width, width, 0, width, 1.0)
    fine_real, fine_imag = complex_mix(
        "vq,cujv->cujq", inner_real, inner_imag, spectrum_real, spectrum_imag
    )
    shift_real, shift_imag = phase_table(blocks, width, 0, tokens, 1.0)
    shift_real = shift_real[None, :, None, :]
    shift_imag = shift_imag[None, :, None, :]
    untwisted_real = fine_real * shift_real - fine_imag * shift_imag
    untwisted_imag = fine_real * shift_imag + fine_imag * shift_real
    outer_real, outer_imag = phase_table(blocks, blocks, 0, blocks, 1.0)
    return complex_mix("ru,cujq->crjq", outer_real, outer_imag, untwisted_real, untwisted_imag)


def forward_spectrum(signal):
    count, tokens = signal.shape
    blocks = lax.axis_size("seq")
    width = tokens // blocks
    freqs = 2 * blocks
    period = freqs * tokens
    rank = lax.axis_index("seq")
    gathered = regroup_tokens(signal.reshape(count, blocks, width))
    product = partial(jnp.einsum, "kp,cpq->ckq", precision=lax.Precision.HIGHEST)
    anchor = rank * width
    first_real, first_imag = phase_table(freqs, blocks, 0, freqs, -1.0)
    mixed_real = product(first_real, gathered)
    mixed_imag = product(first_imag, gathered)
    turn_real, turn_imag = phase_table(freqs, width, anchor, period, -1.0)
    moved_real, moved_imag = regroup_spectrum(
        mixed_real * turn_real - mixed_imag * turn_imag,
        mixed_real * turn_imag + mixed_imag * turn_real,
    )
    moved_real = moved_real.reshape(count, blocks, 2, width)
    moved_imag = moved_imag.reshape(count, blocks, 2, width)
    return finish_forward(moved_real, moved_imag, blocks, width, tokens)


def inverse_spectrum(spectrum_real, spectrum_imag):
    count, blocks, per_device, width = spectrum_real.shape
    tokens = blocks * width
    freqs = 2 * blocks
    period = freqs * tokens
    rank = lax.axis_index("seq")
    spread_real, spread_imag = start_inverse(spectrum_real, spectrum_imag, blocks, width, tokens)
    product = partial(jnp.einsum, "kp,ckq->cpq", precision=lax.Precision.HIGHEST)
    anchor = rank * width
    moved_real, moved_imag = regroup_spectrum(
        spread_real.reshape(count, blocks * per_device, width),
        spread_imag.reshape(count, blocks * per_device, width),
    )
    turn_real, turn_imag = phase_table(freqs, width, anchor, period, 1.0)
    level_real = moved_real * turn_real - moved_imag * turn_imag
    level_imag = moved_real * turn_imag + moved_imag * turn_real
    first_real, first_imag = phase_table(freqs, blocks, 0, freqs, 1.0)
    rebuilt = (product(first_real, level_real) - product(first_imag, level_imag)) * (1.0 / period)
    return regroup_tokens(rebuilt).reshape(count, tokens)


def on_device(query_gate, key_gate, value_input, filter_taps, cotangent):
    if one_row_each(query_gate, filter_taps):
        return rows_on_device(query_gate, key_gate, value_input, filter_taps, cotangent)
    block_taps = lax.all_gather(filter_taps, "chan", axis=1, tiled=True)
    filter_real, filter_imag = forward_spectrum(block_taps)
    gated = key_gate * value_input
    weighted = cotangent * query_gate
    gated_real, gated_imag = forward_spectrum(gated)
    convolved = inverse_spectrum(
        gated_real * filter_real - gated_imag * filter_imag,
        gated_real * filter_imag + gated_imag * filter_real,
    )
    weighted_real, weighted_imag = forward_spectrum(weighted)
    gated_grad = inverse_spectrum(
        weighted_real * filter_real + weighted_imag * filter_imag,
        weighted_imag * filter_real - weighted_real * filter_imag,
    )
    return (cotangent * convolved, gated_grad * value_input, gated_grad * key_gate)


def solution(mesh):
    in_specs = (
        P("chan", "seq"),
        P("chan", "seq"),
        P("chan", "seq"),
        P(None, ("seq", "chan")),
        P("chan", "seq"),
    )
    out_specs = (P("chan", "seq"), P("chan", "seq"), P("chan", "seq"))
    return jax.shard_map(
        on_device, mesh=mesh, in_specs=in_specs, out_specs=out_specs, check_vma=False
    )
```

```python
from functools import partial
import math

import jax
import jax.numpy as jnp
import numpy as np
from jax import lax
from jax.experimental import pallas as pl
from jax.experimental.pallas import tpu as pltpu
from jax.sharding import PartitionSpec as P

MESH = pl.DeviceIdType.MESH
SIDE = 256
LANES = 128
VMEM_BYTES = 63 * 1024 * 1024


def fourier_tables():
    total = SIDE * SIDE
    index = np.arange(SIDE, dtype=np.float64)
    outer = 2.0 * np.pi * np.outer(index + 0.25, index) / SIDE
    first = np.concatenate([np.cos(outer), -np.sin(outer)], axis=0)
    last = first.T / total
    inner = 2.0 * np.pi * (np.outer(index, index) % SIDE) / SIDE
    twist = 2.0 * np.pi * np.outer(index + 0.25, index) / total
    tables = (first, np.cos(inner), np.sin(inner), last, np.cos(twist), -np.sin(twist))
    return tuple(table.astype(np.float32) for table in tables)


def split(value):
    high = value.astype(jnp.bfloat16)
    low = (value - high.astype(jnp.float32)).astype(jnp.bfloat16)
    return high, low


def mul(left, right):
    dot = partial(jnp.dot, preferred_element_type=jnp.float32)
    return dot(left[0], right[0]) + (dot(left[0], right[1]) + dot(left[1], right[0]))


def row_kernel(
    blocks, groups, k_hbm, v_hbm, q_hbm, c_hbm, taps_hbm,
    first_hbm, cos_hbm, sin_hbm, last_hbm, turn_re_hbm, turn_im_hbm, out_ref,
    k_ref, v_ref, q_ref, c_ref, taps_ref, first_ref, cos_ref, sin_ref, last_ref, turn_re_ref, turn_im_ref,
    pieces, tap_pieces, rows, filt, result, back,
    first_hi, first_lo, mid_hi, mid_lo, inv_hi, inv_lo, last_hi, last_lo,
    load_sem, tap_send, tap_recv, slab_send, slab_recv, in_send, in_recv, out_send, out_recv,
):
    me = lax.axis_index("seq")
    col = lax.axis_index("chan")
    count = k_ref.shape[0]
    parts = SIDE // LANES

    sources = (taps_hbm, k_hbm, v_hbm, c_hbm, q_hbm, first_hbm, cos_hbm, sin_hbm, turn_re_hbm, turn_im_hbm, last_hbm)
    targets = (taps_ref, k_ref, v_ref, c_ref, q_ref, first_ref, cos_ref, sin_ref, turn_re_ref, turn_im_ref, last_ref)
    loads = [
        pltpu.make_async_copy(source, target, load_sem.at[place])
        for place, (source, target) in enumerate(zip(sources, targets))
    ]
    for load in loads:
        load.start()

    barrier = pltpu.get_barrier_semaphore()
    for step in range(1, blocks):
        pl.semaphore_signal(barrier, inc=1, device_id=(lax.rem(me + step, blocks), col), device_id_type=MESH)
    for step in range(1, groups):
        pl.semaphore_signal(barrier, inc=1, device_id=(me, lax.rem(col + step, groups)), device_id_type=MESH)

    def span(row, part):
        return slice(row * SIDE + part * LANES, row * SIDE + (part + 1) * LANES)

    loads[0].wait()
    for part in range(parts):
        for row in range(taps_ref.shape[1] // SIDE):
            tap_pieces[:, part, row, :] = taps_ref[:, span(row, part)]
    for load in loads[1:5]:
        load.wait()
    for part in range(parts):
        for row in range(k_ref.shape[1] // SIDE):
            tokens = span(row, part)
            pieces[:count, part, row, :] = k_ref[:, tokens] * v_ref[:, tokens]
            pieces[count:, part, row, :] = c_ref[:, tokens] * q_ref[:, tokens]

    pl.semaphore_wait(barrier, blocks + groups - 2)

    tap_copies, slab_copies = [], []
    in_copies, out_copies = [[] for _ in range(parts)], [[] for _ in range(parts)]
    for step in range(1, blocks):
        target = lax.rem(me + step, blocks)
        copy = pltpu.make_async_remote_copy(
            src_ref=tap_pieces.at[lax.rem(target, count)], dst_ref=filt.at[me, col],
            send_sem=tap_send.at[step], recv_sem=tap_recv.at[step],
            device_id=(target, col), device_id_type=MESH,
        )
        copy.start()
        tap_copies.append(copy)
    for part in range(parts):
        for step in range(1, blocks):
            target = lax.rem(me + step, blocks)
            copy = pltpu.make_async_remote_copy(
                src_ref=pieces.at[target, part], dst_ref=rows.at[part, me],
                send_sem=in_send.at[part, step], recv_sem=in_recv.at[part, step],
                device_id=(target, col), device_id_type=MESH,
            )
            copy.start()
            in_copies[part].append(copy)
    filt[me, col] = tap_pieces[lax.rem(me, count)]
    for part in range(parts):
        rows[part, me] = pieces[me, part]

    for copy in tap_copies:
        copy.wait_recv()
    for step in range(1, groups):
        copy = pltpu.make_async_remote_copy(
            src_ref=filt.at[:, col], dst_ref=filt.at[:, col],
            send_sem=slab_send.at[step], recv_sem=slab_recv.at[step],
            device_id=(me, lax.rem(col + step, groups)), device_id_type=MESH,
        )
        copy.start()
        slab_copies.append(copy)

    for load in loads[5:]:
        load.wait()
    first_hi[...], first_lo[...] = split(first_ref[...])
    last_hi[...], last_lo[...] = split(last_ref[...])
    cosines, sines = split(cos_ref[...]), split(sin_ref[...])
    for part in range(parts):
        cut = slice(part * LANES, (part + 1) * LANES)
        real_rows = slice(2 * part * LANES, (2 * part + 1) * LANES)
        imag_rows = slice((2 * part + 1) * LANES, (2 * part + 2) * LANES)
        for mid, inv, cosine, sine in zip((mid_hi, mid_lo), (inv_hi, inv_lo), cosines, sines):
            mid[real_rows, :SIDE] = cosine[cut]
            mid[real_rows, SIDE:] = -sine[cut]
            mid[imag_rows, :SIDE] = sine[cut]
            mid[imag_rows, SIDE:] = cosine[cut]
            inv[part, :SIDE, :LANES] = cosine[:, cut]
            inv[part, :SIDE, LANES:] = sine[:, cut]
            inv[part, SIDE:, :LANES] = -sine[:, cut]
            inv[part, SIDE:, LANES:] = cosine[:, cut]

    def part_spectrum(part, signal):
        cut = slice(part * LANES, (part + 1) * LANES)
        wide = slice(part * SIDE, (part + 1) * SIDE)
        mixed = mul((first_hi[...], first_lo[...]), split(signal))
        real, imag = mixed[:SIDE], mixed[SIDE:]
        turn_re, turn_im = turn_re_ref[:, cut], turn_im_ref[:, cut]
        twisted = jnp.concatenate(
            [real * turn_re - imag * turn_im, real * turn_im + imag * turn_re], axis=1
        )
        return mul(split(twisted), (mid_hi[wide], mid_lo[wide]))

    def row_spectrum(part):
        for copy in in_copies[part]:
            copy.wait_recv()
        return part_spectrum(part, rows[part].reshape(SIDE, LANES))

    row_total = row_spectrum(0)
    for copy in slab_copies:
        copy.wait_recv()
    tap_total = part_spectrum(0, filt[:, :, 0].reshape(SIDE, LANES))
    for part in range(1, parts):
        tap_total += part_spectrum(part, filt[:, :, part].reshape(SIDE, LANES))
    tap_re = tap_total[:, :SIDE]
    tap_im = tap_total[:, SIDE:] * jnp.where(me < count, 1.0, -1.0)
    for part in range(1, parts):
        row_total += row_spectrum(part)
    row_re, row_im = row_total[:, :SIDE], row_total[:, SIDE:]
    joined = split(jnp.concatenate(
        [row_re * tap_re - row_im * tap_im, row_re * tap_im + row_im * tap_re], axis=1
    ))
    for part in range(parts):
        cut = slice(part * LANES, (part + 1) * LANES)
        coarse = mul(joined, (inv_hi[part], inv_lo[part]))
        real, imag = coarse[:, :LANES], coarse[:, LANES:]
        turn_re, turn_im = turn_re_ref[:, cut], turn_im_ref[:, cut]
        level = jnp.concatenate(
            [real * turn_re + imag * turn_im, imag * turn_re - real * turn_im], axis=0
        )
        rebuilt = mul((last_hi[...], last_lo[...]), split(level))
        result[part] = rebuilt.reshape(result.shape[1:])
        for step in range(1, blocks):
            target = lax.rem(me + step, blocks)
            copy = pltpu.make_async_remote_copy(
                src_ref=result.at[part, target], dst_ref=back.at[me, part],
                send_sem=out_send.at[part, step], recv_sem=out_recv.at[part, step],
                device_id=(target, col), device_id_type=MESH,
            )
            copy.start()
            out_copies[part].append(copy)
        back[me, part] = result[part, me]
    for part in range(parts):
        for copy in out_copies[part]:
            copy.wait_recv()
        for row in range(back.shape[2]):
            out_ref[:, span(row, part)] = back[:, part, row, :]
    for copy in tap_copies + sum(in_copies, []) + slab_copies + sum(out_copies, []):
        copy.wait_send()


def rows_on_device(query_gate, key_gate, value_input, filter_taps, cotangent):
    count, width = query_gate.shape
    blocks = lax.axis_size("seq")
    groups = lax.axis_size("chan")
    high = width // SIDE
    parts = SIDE // LANES
    tables = fourier_tables()
    f32, bf16 = jnp.float32, jnp.bfloat16
    operands = (key_gate, value_input, query_gate, cotangent, filter_taps, *[jnp.asarray(table) for table in tables])
    sums = pl.pallas_call(
        partial(row_kernel, blocks, groups),
        out_shape=jax.ShapeDtypeStruct((blocks, width), f32),
        in_specs=[pl.BlockSpec(memory_space=pl.ANY)] * len(operands),
        out_specs=pl.BlockSpec(memory_space=pltpu.VMEM),
        scratch_shapes=[
            *[pltpu.VMEM(operand.shape, f32) for operand in operands],
            pltpu.VMEM((blocks, parts, high, LANES), f32),
            pltpu.VMEM((count, parts, high // groups, LANES), f32),
            pltpu.VMEM((parts, blocks, high, LANES), f32),
            pltpu.VMEM((blocks, groups, parts, high // groups, LANES), f32),
            pltpu.VMEM((parts, blocks, high, LANES), f32),
            pltpu.VMEM((blocks, parts, high, LANES), f32),
            pltpu.VMEM((2 * SIDE, SIDE), bf16),
            pltpu.VMEM((2 * SIDE, SIDE), bf16),
            pltpu.VMEM((2 * SIDE, 2 * SIDE), bf16),
            pltpu.VMEM((2 * SIDE, 2 * SIDE), bf16),
            pltpu.VMEM((parts, 2 * SIDE, SIDE), bf16),
            pltpu.VMEM((parts, 2 * SIDE, SIDE), bf16),
            pltpu.VMEM((SIDE, 2 * SIDE), bf16),
            pltpu.VMEM((SIDE, 2 * SIDE), bf16),
            pltpu.SemaphoreType.DMA((len(operands),)),
            pltpu.SemaphoreType.DMA((blocks,)),
            pltpu.SemaphoreType.DMA((blocks,)),
            pltpu.SemaphoreType.DMA((groups,)),
            pltpu.SemaphoreType.DMA((groups,)),
            pltpu.SemaphoreType.DMA((parts, blocks)),
            pltpu.SemaphoreType.DMA((parts, blocks)),
            pltpu.SemaphoreType.DMA((parts, blocks)),
            pltpu.SemaphoreType.DMA((parts, blocks)),
        ],
        compiler_params=pltpu.CompilerParams(
            collective_id=0, has_side_effects=True, vmem_limit_bytes=VMEM_BYTES
        ),
    )(*operands)
    convolved, gated_grad = sums[:count], sums[count:]
    return (cotangent * convolved, gated_grad * value_input, gated_grad * key_gate)


def one_row_each(query_gate, filter_taps):
    count, width = query_gate.shape
    blocks = lax.axis_size("seq")
    groups = lax.axis_size("chan")
    return (
        blocks == 2 * count
        and filter_taps.shape[0] == count
        and blocks * width == SIDE * SIDE
        and width % (8 * groups * SIDE) == 0
    )


def phase_table(row_count, column_count, offset, period, direction):
    row_index = lax.broadcasted_iota(jnp.int32, (row_count, column_count), 0)
    column_index = lax.broadcasted_iota(jnp.int32, (row_count, column_count), 1)
    phases = row_index * (column_index + offset) % period
    angles = phases.astype(jnp.float32) * (direction * 2.0 * math.pi / period)
    return (jnp.cos(angles), jnp.sin(angles))


def complex_mix(formula, table_real, table_imag, data_real, data_imag):
    product = partial(jnp.einsum, formula, precision=lax.Precision.HIGHEST)
    return (
        product(table_real, data_real) - product(table_imag, data_imag),
        product(table_real, data_imag) + product(table_imag, data_real),
    )


def regroup_tokens(signal):
    return lax.all_to_all(signal, "seq", split_axis=1, concat_axis=1, tiled=True)


def regroup_spectrum(part_real, part_imag):
    return (
        lax.all_to_all(part_real, "seq", split_axis=1, concat_axis=1, tiled=True),
        lax.all_to_all(part_imag, "seq", split_axis=1, concat_axis=1, tiled=True),
    )


def finish_forward(moved_real, moved_imag, blocks, width, tokens):
    outer_real, outer_imag = phase_table(blocks, blocks, 0, blocks, -1.0)
    coarse_real, coarse_imag = complex_mix(
        "ur,crjq->cujq", outer_real, outer_imag, moved_real, moved_imag
    )
    shift_real, shift_imag = phase_table(blocks, width, 0, tokens, -1.0)
    shift_real = shift_real[None, :, None, :]
    shift_imag = shift_imag[None, :, None, :]
    twisted_real = coarse_real * shift_real - coarse_imag * shift_imag
    twisted_imag = coarse_real * shift_imag + coarse_imag * shift_real
    inner_real, inner_imag = phase_table(width, width, 0, width, -1.0)
    return complex_mix("qv,cujq->cujv", inner_real, inner_imag, twisted_real, twisted_imag)


def start_inverse(spectrum_real, spectrum_imag, blocks, width, tokens):
    inner_real, inner_imag = phase_table(width, width, 0, width, 1.0)
    fine_real, fine_imag = complex_mix(
        "vq,cujv->cujq", inner_real, inner_imag, spectrum_real, spectrum_imag
    )
    shift_real, shift_imag = phase_table(blocks, width, 0, tokens, 1.0)
    shift_real = shift_real[None, :, None, :]
    shift_imag = shift_imag[None, :, None, :]
    untwisted_real = fine_real * shift_real - fine_imag * shift_imag
    untwisted_imag = fine_real * shift_imag + fine_imag * shift_real
    outer_real, outer_imag = phase_table(blocks, blocks, 0, blocks, 1.0)
    return complex_mix("ru,cujq->crjq", outer_real, outer_imag, untwisted_real, untwisted_imag)


def forward_spectrum(signal):
    count, tokens = signal.shape
    blocks = lax.axis_size("seq")
    width = tokens // blocks
    freqs = 2 * blocks
    period = freqs * tokens
    rank = lax.axis_index("seq")
    gathered = regroup_tokens(signal.reshape(count, blocks, width))
    product = partial(jnp.einsum, "kp,cpq->ckq", precision=lax.Precision.HIGHEST)
    anchor = rank * width
    first_real, first_imag = phase_table(freqs, blocks, 0, freqs, -1.0)
    mixed_real = product(first_real, gathered)
    mixed_imag = product(first_imag, gathered)
    turn_real, turn_imag = phase_table(freqs, width, anchor, period, -1.0)
    moved_real, moved_imag = regroup_spectrum(
        mixed_real * turn_real - mixed_imag * turn_imag,
        mixed_real * turn_imag + mixed_imag * turn_real,
    )
    moved_real = moved_real.reshape(count, blocks, 2, width)
    moved_imag = moved_imag.reshape(count, blocks, 2, width)
    return finish_forward(moved_real, moved_imag, blocks, width, tokens)


def inverse_spectrum(spectrum_real, spectrum_imag):
    count, blocks, per_device, width = spectrum_real.shape
    tokens = blocks * width
    freqs = 2 * blocks
    period = freqs * tokens
    rank = lax.axis_index("seq")
    spread_real, spread_imag = start_inverse(spectrum_real, spectrum_imag, blocks, width, tokens)
    product = partial(jnp.einsum, "kp,ckq->cpq", precision=lax.Precision.HIGHEST)
    anchor = rank * width
    moved_real, moved_imag = regroup_spectrum(
        spread_real.reshape(count, blocks * per_device, width),
        spread_imag.reshape(count, blocks * per_device, width),
    )
    turn_real, turn_imag = phase_table(freqs, width, anchor, period, 1.0)
    level_real = moved_real * turn_real - moved_imag * turn_imag
    level_imag = moved_real * turn_imag + moved_imag * turn_real
    first_real, first_imag = phase_table(freqs, blocks, 0, freqs, 1.0)
    rebuilt = (product(first_real, level_real) - product(first_imag, level_imag)) * (1.0 / period)
    return regroup_tokens(rebuilt).reshape(count, tokens)


def on_device(query_gate, key_gate, value_input, filter_taps, cotangent):
    if one_row_each(query_gate, filter_taps):
        return rows_on_device(query_gate, key_gate, value_input, filter_taps, cotangent)
    block_taps = lax.all_gather(filter_taps, "chan", axis=1, tiled=True)
    filter_real, filter_imag = forward_spectrum(block_taps)
    gated = key_gate * value_input
    weighted = cotangent * query_gate
    gated_real, gated_imag = forward_spectrum(gated)
    convolved = inverse_spectrum(
        gated_real * filter_real - gated_imag * filter_imag,
        gated_real * filter_imag + gated_imag * filter_real,
    )
    weighted_real, weighted_imag = forward_spectrum(weighted)
    gated_grad = inverse_spectrum(
        weighted_real * filter_real + weighted_imag * filter_imag,
        weighted_imag * filter_real - weighted_real * filter_imag,
    )
    return (cotangent * convolved, gated_grad * value_input, gated_grad * key_gate)


def solution(mesh):
    in_specs = (
        P("chan", "seq"),
        P("chan", "seq"),
        P("chan", "seq"),
        P(None, ("seq", "chan")),
        P("chan", "seq"),
    )
    out_specs = (P("chan", "seq"), P("chan", "seq"), P("chan", "seq"))
    return jax.shard_map(
        on_device, mesh=mesh, in_specs=in_specs, out_specs=out_specs, check_vma=False
    )
```

```python
from functools import partial
import math

import jax
import jax.numpy as jnp
import numpy as np
from jax import lax
from jax.experimental import pallas as pl
from jax.experimental.pallas import tpu as pltpu
from jax.sharding import PartitionSpec as P

MESH = pl.DeviceIdType.MESH
SIDE = 256
LANES = 128
VMEM_BYTES = 63 * 1024 * 1024


def fourier_tables():
    total = SIDE * SIDE
    index = np.arange(SIDE, dtype=np.float64)
    outer = 2.0 * np.pi * np.outer(index + 0.25, index) / SIDE
    first = np.concatenate([np.cos(outer), -np.sin(outer)], axis=0)
    last = first.T / total
    inner = 2.0 * np.pi * (np.outer(index, index) % SIDE) / SIDE
    twist = 2.0 * np.pi * np.outer(index + 0.25, index) / total
    tables = (first, np.cos(inner), np.sin(inner), last, np.cos(twist), -np.sin(twist))
    return tuple(table.astype(np.float32) for table in tables)


def split(value):
    high = value.astype(jnp.bfloat16)
    low = (value - high.astype(jnp.float32)).astype(jnp.bfloat16)
    return high, low


def mul(left, right):
    dot = partial(jnp.dot, preferred_element_type=jnp.float32)
    return dot(left[0], right[0]) + (dot(left[0], right[1]) + dot(left[1], right[0]))


def row_kernel(
    blocks, groups, k_hbm, v_hbm, q_hbm, c_hbm, taps_hbm,
    first_hbm, cos_hbm, sin_hbm, last_hbm, turn_re_hbm, turn_im_hbm, out_ref,
    k_ref, v_ref, q_ref, c_ref, taps_ref, first_ref, cos_ref, sin_ref, last_ref, turn_re_ref, turn_im_ref,
    pieces, tap_pieces, rows, side, filt, result, side_result, back,
    first_hi, first_lo, mid_hi, mid_lo, inv_hi, inv_lo, last_hi, last_lo,
    load_sem, tap_send, tap_recv, slab_send, slab_recv, in_send, in_recv, out_send, out_recv,
    side_send, side_recv, home_send, home_recv,
):
    me = lax.axis_index("seq")
    col = lax.axis_index("chan")
    count = k_ref.shape[0]
    parts = SIDE // LANES
    near = blocks // 2
    base = (me // near) * near
    local = lax.rem(me, near)
    depth = SIDE // 2

    sources = (taps_hbm, k_hbm, v_hbm, c_hbm, q_hbm, first_hbm, cos_hbm, sin_hbm, turn_re_hbm, turn_im_hbm, last_hbm)
    targets = (taps_ref, k_ref, v_ref, c_ref, q_ref, first_ref, cos_ref, sin_ref, turn_re_ref, turn_im_ref, last_ref)
    loads = [
        pltpu.make_async_copy(source, target, load_sem.at[place])
        for place, (source, target) in enumerate(zip(sources, targets))
    ]
    for load in loads:
        load.start()

    barrier = pltpu.get_barrier_semaphore()
    for step in range(1, blocks):
        pl.semaphore_signal(barrier, inc=1, device_id=(lax.rem(me + step, blocks), col), device_id_type=MESH)
    for step in range(1, groups):
        pl.semaphore_signal(barrier, inc=1, device_id=(me, lax.rem(col + step, groups)), device_id_type=MESH)

    def span(row, part):
        return slice(row * SIDE + part * LANES, row * SIDE + (part + 1) * LANES)

    loads[0].wait()
    for part in range(parts):
        for row in range(taps_ref.shape[1] // SIDE):
            tap_pieces[:, part, row, :] = taps_ref[:, span(row, part)]
    for load in loads[1:5]:
        load.wait()
    for part in range(parts):
        for row in range(k_ref.shape[1] // SIDE):
            tokens = span(row, part)
            pieces[:count, part, row, :] = k_ref[:, tokens] * v_ref[:, tokens]
            pieces[count:, part, row, :] = c_ref[:, tokens] * q_ref[:, tokens]

    pl.semaphore_wait(barrier, blocks + groups - 2)

    tap_copies, slab_copies, side_copies, home_copies = [], [], [], []
    in_copies, out_copies = [[] for _ in range(parts)], [[] for _ in range(parts)]
    for step in range(1, blocks):
        target = lax.rem(me + step, blocks)
        copy = pltpu.make_async_remote_copy(
            src_ref=tap_pieces.at[lax.rem(target, count)], dst_ref=filt.at[me, col],
            send_sem=tap_send.at[step], recv_sem=tap_recv.at[step],
            device_id=(target, col), device_id_type=MESH,
        )
        copy.start()
        tap_copies.append(copy)
    for part in range(parts):
        for step in range(1, blocks):
            target = lax.rem(me + step, blocks)
            copy = pltpu.make_async_remote_copy(
                src_ref=pieces.at[lax.rem(target + near, blocks), part], dst_ref=rows.at[part, me],
                send_sem=in_send.at[part, step], recv_sem=in_recv.at[part, step],
                device_id=(target, col), device_id_type=MESH,
            )
            copy.start()
            in_copies[part].append(copy)
        for step in range(1, near if part == 0 else 1):
            target = base + lax.rem(me + step, near)
            copy = pltpu.make_async_remote_copy(
                src_ref=pieces.at[target], dst_ref=side.at[local],
                send_sem=side_send.at[step], recv_sem=side_recv.at[step],
                device_id=(target, col), device_id_type=MESH,
            )
            copy.start()
            side_copies.append(copy)
    side[local] = pieces[me]
    filt[me, col] = tap_pieces[lax.rem(me, count)]
    for part in range(parts):
        rows[part, me] = pieces[lax.rem(me + near, blocks), part]

    for copy in tap_copies:
        copy.wait_recv()
    for step in range(1, groups):
        copy = pltpu.make_async_remote_copy(
            src_ref=filt.at[:, col], dst_ref=filt.at[:, col],
            send_sem=slab_send.at[step], recv_sem=slab_recv.at[step],
            device_id=(me, lax.rem(col + step, groups)), device_id_type=MESH,
        )
        copy.start()
        slab_copies.append(copy)

    for load in loads[5:]:
        load.wait()
    first_hi[...], first_lo[...] = split(first_ref[...])
    last_hi[...], last_lo[...] = split(last_ref[...])
    cosines, sines = split(cos_ref[...]), split(sin_ref[...])
    for part in range(parts):
        cut = slice(part * LANES, (part + 1) * LANES)
        real_rows = slice(2 * part * LANES, (2 * part + 1) * LANES)
        imag_rows = slice((2 * part + 1) * LANES, (2 * part + 2) * LANES)
        for mid, inv, cosine, sine in zip((mid_hi, mid_lo), (inv_hi, inv_lo), cosines, sines):
            mid[real_rows, :SIDE] = cosine[cut]
            mid[real_rows, SIDE:] = -sine[cut]
            mid[imag_rows, :SIDE] = sine[cut]
            mid[imag_rows, SIDE:] = cosine[cut]
            inv[part, :SIDE, :LANES] = cosine[:, cut]
            inv[part, :SIDE, LANES:] = sine[:, cut]
            inv[part, SIDE:, :LANES] = -sine[:, cut]
            inv[part, SIDE:, LANES:] = cosine[:, cut]

    def part_spectrum(part, signal):
        cut = slice(part * LANES, (part + 1) * LANES)
        wide = slice(part * SIDE, (part + 1) * SIDE)
        held = slice(0, signal.shape[0])
        mixed = mul((first_hi[:, held], first_lo[:, held]), split(signal))
        real, imag = mixed[:SIDE], mixed[SIDE:]
        turn_re, turn_im = turn_re_ref[:, cut], turn_im_ref[:, cut]
        twisted = jnp.concatenate(
            [real * turn_re - imag * turn_im, real * turn_im + imag * turn_re], axis=1
        )
        return mul(split(twisted), (mid_hi[wide], mid_lo[wide]))

    def row_spectrum(part):
        for copy in in_copies[part]:
            copy.wait_recv()
        return part_spectrum(part, rows[part].reshape(SIDE, LANES))

    def product(total, tap_re, tap_im):
        real, imag = total[:, :SIDE], total[:, SIDE:]
        return split(jnp.concatenate([real * tap_re - imag * tap_im, real * tap_im + imag * tap_re], axis=1))

    def part_tokens(part, joined, first_row):
        cut = slice(part * LANES, (part + 1) * LANES)
        coarse = mul(joined, (inv_hi[part], inv_lo[part]))
        real, imag = coarse[:, :LANES], coarse[:, LANES:]
        turn_re, turn_im = turn_re_ref[:, cut], turn_im_ref[:, cut]
        level = jnp.concatenate(
            [real * turn_re + imag * turn_im, imag * turn_re - real * turn_im], axis=0
        )
        kept = pl.ds(first_row, depth)
        return mul((last_hi[kept, :], last_lo[kept, :]), split(level))

    row_total = row_spectrum(0)
    for copy in slab_copies:
        copy.wait_recv()
    tap_total = part_spectrum(0, filt[:, :, 0].reshape(SIDE, LANES))
    for part in range(1, parts):
        tap_total += part_spectrum(part, filt[:, :, part].reshape(SIDE, LANES))
    tap_re = tap_total[:, :SIDE]
    tap_im = tap_total[:, SIDE:] * jnp.where(me < near, -1.0, 1.0)

    for copy in side_copies:
        copy.wait_recv()
    side_total = part_spectrum(0, side[:, 0].reshape(depth, LANES))
    for part in range(1, parts):
        side_total += part_spectrum(part, side[:, part].reshape(depth, LANES))
    joined = product(side_total, tap_re, -tap_im)
    for part in range(parts):
        side_result[:, part] = part_tokens(part, joined, 0).reshape(near, *side_result.shape[2:])
    for step in range(1, near):
        target = lax.rem(me + step, near)
        copy = pltpu.make_async_remote_copy(
            src_ref=side_result.at[target], dst_ref=back.at[me],
            send_sem=home_send.at[step], recv_sem=home_recv.at[step],
            device_id=(base + target, col), device_id_type=MESH,
        )
        copy.start()
        home_copies.append(copy)
    back[me] = side_result[local]

    for part in range(1, parts):
        row_total += row_spectrum(part)
    joined = product(row_total, tap_re, tap_im)
    place = lax.rem(me + near, blocks)
    for part in range(parts):
        result[part] = part_tokens(part, joined, pl.multiple_of((me // near) * depth, depth)).reshape(result.shape[1:])
        for step in range(1, near):
            target = lax.rem(me + step, near)
            copy = pltpu.make_async_remote_copy(
                src_ref=result.at[part, target], dst_ref=back.at[place, part],
                send_sem=out_send.at[part, step], recv_sem=out_recv.at[part, step],
                device_id=(base + target, col), device_id_type=MESH,
            )
            copy.start()
            out_copies[part].append(copy)
        back[place, part] = result[part, local]
    for copy in home_copies:
        copy.wait_recv()
    for part in range(parts):
        for copy in out_copies[part]:
            copy.wait_recv()
        for row in range(back.shape[2]):
            out_ref[:, span(row, part)] = back[:, part, row, :]
    for copy in tap_copies + sum(in_copies, []) + slab_copies + side_copies + home_copies + sum(out_copies, []):
        copy.wait_send()


def rows_on_device(query_gate, key_gate, value_input, filter_taps, cotangent):
    count, width = query_gate.shape
    blocks = lax.axis_size("seq")
    groups = lax.axis_size("chan")
    high = width // SIDE
    near = blocks // 2
    parts = SIDE // LANES
    tables = fourier_tables()
    f32, bf16 = jnp.float32, jnp.bfloat16
    operands = (key_gate, value_input, query_gate, cotangent, filter_taps, *[jnp.asarray(table) for table in tables])
    sums = pl.pallas_call(
        partial(row_kernel, blocks, groups),
        out_shape=jax.ShapeDtypeStruct((blocks, width), f32),
        in_specs=[pl.BlockSpec(memory_space=pl.ANY)] * len(operands),
        out_specs=pl.BlockSpec(memory_space=pltpu.VMEM),
        scratch_shapes=[
            *[pltpu.VMEM(operand.shape, f32) for operand in operands],
            pltpu.VMEM((blocks, parts, high, LANES), f32),
            pltpu.VMEM((count, parts, high // groups, LANES), f32),
            pltpu.VMEM((parts, blocks, high, LANES), f32),
            pltpu.VMEM((near, parts, high, LANES), f32),
            pltpu.VMEM((blocks, groups, parts, high // groups, LANES), f32),
            pltpu.VMEM((parts, near, high, LANES), f32),
            pltpu.VMEM((near, parts, high, LANES), f32),
            pltpu.VMEM((blocks, parts, high, LANES), f32),
            pltpu.VMEM((2 * SIDE, SIDE), bf16),
            pltpu.VMEM((2 * SIDE, SIDE), bf16),
            pltpu.VMEM((2 * SIDE, 2 * SIDE), bf16),
            pltpu.VMEM((2 * SIDE, 2 * SIDE), bf16),
            pltpu.VMEM((parts, 2 * SIDE, SIDE), bf16),
            pltpu.VMEM((parts, 2 * SIDE, SIDE), bf16),
            pltpu.VMEM((SIDE, 2 * SIDE), bf16),
            pltpu.VMEM((SIDE, 2 * SIDE), bf16),
            pltpu.SemaphoreType.DMA((len(operands),)),
            pltpu.SemaphoreType.DMA((blocks,)),
            pltpu.SemaphoreType.DMA((blocks,)),
            pltpu.SemaphoreType.DMA((groups,)),
            pltpu.SemaphoreType.DMA((groups,)),
            pltpu.SemaphoreType.DMA((parts, blocks)),
            pltpu.SemaphoreType.DMA((parts, blocks)),
            pltpu.SemaphoreType.DMA((parts, blocks)),
            pltpu.SemaphoreType.DMA((parts, blocks)),
            *[pltpu.SemaphoreType.DMA((near,))] * 4,
        ],
        compiler_params=pltpu.CompilerParams(
            collective_id=0, has_side_effects=True, vmem_limit_bytes=VMEM_BYTES
        ),
    )(*operands)
    convolved, gated_grad = sums[:count], sums[count:]
    return (cotangent * convolved, gated_grad * value_input, gated_grad * key_gate)


def one_row_each(query_gate, filter_taps):
    count, width = query_gate.shape
    blocks = lax.axis_size("seq")
    groups = lax.axis_size("chan")
    return (
        blocks == 2 * count
        and filter_taps.shape[0] == count
        and blocks * width == SIDE * SIDE
        and width % (8 * groups * SIDE) == 0
    )


def phase_table(row_count, column_count, offset, period, direction):
    row_index = lax.broadcasted_iota(jnp.int32, (row_count, column_count), 0)
    column_index = lax.broadcasted_iota(jnp.int32, (row_count, column_count), 1)
    phases = row_index * (column_index + offset) % period
    angles = phases.astype(jnp.float32) * (direction * 2.0 * math.pi / period)
    return (jnp.cos(angles), jnp.sin(angles))


def complex_mix(formula, table_real, table_imag, data_real, data_imag):
    product = partial(jnp.einsum, formula, precision=lax.Precision.HIGHEST)
    return (
        product(table_real, data_real) - product(table_imag, data_imag),
        product(table_real, data_imag) + product(table_imag, data_real),
    )


def regroup_tokens(signal):
    return lax.all_to_all(signal, "seq", split_axis=1, concat_axis=1, tiled=True)


def regroup_spectrum(part_real, part_imag):
    return (
        lax.all_to_all(part_real, "seq", split_axis=1, concat_axis=1, tiled=True),
        lax.all_to_all(part_imag, "seq", split_axis=1, concat_axis=1, tiled=True),
    )


def finish_forward(moved_real, moved_imag, blocks, width, tokens):
    outer_real, outer_imag = phase_table(blocks, blocks, 0, blocks, -1.0)
    coarse_real, coarse_imag = complex_mix(
        "ur,crjq->cujq", outer_real, outer_imag, moved_real, moved_imag
    )
    shift_real, shift_imag = phase_table(blocks, width, 0, tokens, -1.0)
    shift_real = shift_real[None, :, None, :]
    shift_imag = shift_imag[None, :, None, :]
    twisted_real = coarse_real * shift_real - coarse_imag * shift_imag
    twisted_imag = coarse_real * shift_imag + coarse_imag * shift_real
    inner_real, inner_imag = phase_table(width, width, 0, width, -1.0)
    return complex_mix("qv,cujq->cujv", inner_real, inner_imag, twisted_real, twisted_imag)


def start_inverse(spectrum_real, spectrum_imag, blocks, width, tokens):
    inner_real, inner_imag = phase_table(width, width, 0, width, 1.0)
    fine_real, fine_imag = complex_mix(
        "vq,cujv->cujq", inner_real, inner_imag, spectrum_real, spectrum_imag
    )
    shift_real, shift_imag = phase_table(blocks, width, 0, tokens, 1.0)
    shift_real = shift_real[None, :, None, :]
    shift_imag = shift_imag[None, :, None, :]
    untwisted_real = fine_real * shift_real - fine_imag * shift_imag
    untwisted_imag = fine_real * shift_imag + fine_imag * shift_real
    outer_real, outer_imag = phase_table(blocks, blocks, 0, blocks, 1.0)
    return complex_mix("ru,cujq->crjq", outer_real, outer_imag, untwisted_real, untwisted_imag)


def forward_spectrum(signal):
    count, tokens = signal.shape
    blocks = lax.axis_size("seq")
    width = tokens // blocks
    freqs = 2 * blocks
    period = freqs * tokens
    rank = lax.axis_index("seq")
    gathered = regroup_tokens(signal.reshape(count, blocks, width))
    product = partial(jnp.einsum, "kp,cpq->ckq", precision=lax.Precision.HIGHEST)
    anchor = rank * width
    first_real, first_imag = phase_table(freqs, blocks, 0, freqs, -1.0)
    mixed_real = product(first_real, gathered)
    mixed_imag = product(first_imag, gathered)
    turn_real, turn_imag = phase_table(freqs, width, anchor, period, -1.0)
    moved_real, moved_imag = regroup_spectrum(
        mixed_real * turn_real - mixed_imag * turn_imag,
        mixed_real * turn_imag + mixed_imag * turn_real,
    )
    moved_real = moved_real.reshape(count, blocks, 2, width)
    moved_imag = moved_imag.reshape(count, blocks, 2, width)
    return finish_forward(moved_real, moved_imag, blocks, width, tokens)


def inverse_spectrum(spectrum_real, spectrum_imag):
    count, blocks, per_device, width = spectrum_real.shape
    tokens = blocks * width
    freqs = 2 * blocks
    period = freqs * tokens
    rank = lax.axis_index("seq")
    spread_real, spread_imag = start_inverse(spectrum_real, spectrum_imag, blocks, width, tokens)
    product = partial(jnp.einsum, "kp,ckq->cpq", precision=lax.Precision.HIGHEST)
    anchor = rank * width
    moved_real, moved_imag = regroup_spectrum(
        spread_real.reshape(count, blocks * per_device, width),
        spread_imag.reshape(count, blocks * per_device, width),
    )
    turn_real, turn_imag = phase_table(freqs, width, anchor, period, 1.0)
    level_real = moved_real * turn_real - moved_imag * turn_imag
    level_imag = moved_real * turn_imag + moved_imag * turn_real
    first_real, first_imag = phase_table(freqs, blocks, 0, freqs, 1.0)
    rebuilt = (product(first_real, level_real) - product(first_imag, level_imag)) * (1.0 / period)
    return regroup_tokens(rebuilt).reshape(count, tokens)


def on_device(query_gate, key_gate, value_input, filter_taps, cotangent):
    if one_row_each(query_gate, filter_taps):
        return rows_on_device(query_gate, key_gate, value_input, filter_taps, cotangent)
    block_taps = lax.all_gather(filter_taps, "chan", axis=1, tiled=True)
    filter_real, filter_imag = forward_spectrum(block_taps)
    gated = key_gate * value_input
    weighted = cotangent * query_gate
    gated_real, gated_imag = forward_spectrum(gated)
    convolved = inverse_spectrum(
        gated_real * filter_real - gated_imag * filter_imag,
        gated_real * filter_imag + gated_imag * filter_real,
    )
    weighted_real, weighted_imag = forward_spectrum(weighted)
    gated_grad = inverse_spectrum(
        weighted_real * filter_real + weighted_imag * filter_imag,
        weighted_imag * filter_real - weighted_real * filter_imag,
    )
    return (cotangent * convolved, gated_grad * value_input, gated_grad * key_gate)


def solution(mesh):
    in_specs = (
        P("chan", "seq"),
        P("chan", "seq"),
        P("chan", "seq"),
        P(None, ("seq", "chan")),
        P("chan", "seq"),
    )
    out_specs = (P("chan", "seq"), P("chan", "seq"), P("chan", "seq"))
    return jax.shard_map(
        on_device, mesh=mesh, in_specs=in_specs, out_specs=out_specs, check_vma=False
    )
```

```python
from functools import partial
import math

import jax
import jax.numpy as jnp
import numpy as np
from jax import lax
from jax.experimental import pallas as pl
from jax.experimental.pallas import tpu as pltpu
from jax.sharding import PartitionSpec as P

MESH = pl.DeviceIdType.MESH
SIDE = 256
LANES = 128
VMEM_BYTES = 63 * 1024 * 1024


def fourier_tables():
    total = SIDE * SIDE
    index = np.arange(SIDE, dtype=np.float64)
    outer = 2.0 * np.pi * np.outer(index + 0.25, index) / SIDE
    first = np.concatenate([np.cos(outer), -np.sin(outer)], axis=0)
    last = first.T / total
    inner_index = np.arange(LANES, dtype=np.float64)
    inner = 2.0 * np.pi * (np.outer(inner_index, inner_index) % LANES) / LANES
    cosine, sine = np.cos(inner), np.sin(inner)
    middle = np.block([[cosine, -sine], [sine, cosine]])
    inverse = np.block([[cosine, sine], [-sine, cosine]])
    twist = 2.0 * np.pi * np.outer(index + 0.25, index) / total
    odd = 2.0 * np.pi * inner_index / SIDE
    shift = np.stack([np.cos(odd), -np.sin(odd)] * 4)
    tables = (first, middle, inverse, last, np.cos(twist), -np.sin(twist), shift)
    return tuple(table.astype(np.float32) for table in tables)


def split(value):
    high = value.astype(jnp.bfloat16)
    low = (value - high.astype(jnp.float32)).astype(jnp.bfloat16)
    return high, low


def stack_left(value, axis=1):
    high, low = split(value)
    return jnp.concatenate([high, high, low], axis=axis)


def stack_right(value, axis=0):
    high, low = split(value)
    return jnp.concatenate([high, low, high], axis=axis)


def mul(left, right):
    return jnp.dot(left, right, preferred_element_type=jnp.float32)


def row_kernel(
    blocks, groups, k_hbm, v_hbm, q_hbm, c_hbm, taps_hbm,
    first_hbm, mid_hbm, inv_hbm, last_hbm, turn_re_hbm, turn_im_hbm, shift_hbm, out_ref,
    k_ref, v_ref, q_ref, c_ref, taps_ref, first_ref, mid_ref, inv_ref, last_ref, turn_re_ref, turn_im_ref, shift_ref,
    pieces, tap_pieces, rows, side, filt, result, side_result, back,
    first_all, mid_all, inv_all, last_all,
    load_sem, tap_send, tap_recv, slab_send, slab_recv, in_send, in_recv, out_send, out_recv,
    side_send, side_recv, home_send, home_recv,
):
    me = lax.axis_index("seq")
    col = lax.axis_index("chan")
    count = k_ref.shape[0]
    parts = SIDE // LANES
    near = blocks // 2
    base = (me // near) * near
    local = lax.rem(me, near)
    depth = SIDE // 2

    sources = (taps_hbm, k_hbm, v_hbm, c_hbm, q_hbm, first_hbm, mid_hbm, inv_hbm, turn_re_hbm, turn_im_hbm, last_hbm, shift_hbm)
    targets = (taps_ref, k_ref, v_ref, c_ref, q_ref, first_ref, mid_ref, inv_ref, turn_re_ref, turn_im_ref, last_ref, shift_ref)
    loads = [
        pltpu.make_async_copy(source, target, load_sem.at[place])
        for place, (source, target) in enumerate(zip(sources, targets))
    ]
    for load in loads:
        load.start()

    barrier = pltpu.get_barrier_semaphore()
    for step in range(1, blocks):
        pl.semaphore_signal(barrier, inc=1, device_id=(lax.rem(me + step, blocks), col), device_id_type=MESH)
    for step in range(1, groups):
        pl.semaphore_signal(barrier, inc=1, device_id=(me, lax.rem(col + step, groups)), device_id_type=MESH)

    def span(row, part):
        return slice(row * SIDE + part * LANES, row * SIDE + (part + 1) * LANES)

    loads[0].wait()
    for part in range(parts):
        for row in range(taps_ref.shape[1] // SIDE):
            tap_pieces[:, part, row, :] = taps_ref[:, span(row, part)]
    for load in loads[1:5]:
        load.wait()
    for part in range(parts):
        for row in range(k_ref.shape[1] // SIDE):
            tokens = span(row, part)
            pieces[:count, part, row, :] = k_ref[:, tokens] * v_ref[:, tokens]
            pieces[count:, part, row, :] = c_ref[:, tokens] * q_ref[:, tokens]

    pl.semaphore_wait(barrier, blocks + groups - 2)

    tap_copies, slab_copies, side_copies, home_copies = [], [], [], []
    in_copies, out_copies = [[] for _ in range(parts)], [[] for _ in range(parts)]
    for step in range(1, blocks):
        target = lax.rem(me + step, blocks)
        copy = pltpu.make_async_remote_copy(
            src_ref=tap_pieces.at[lax.rem(target, count)], dst_ref=filt.at[me, col],
            send_sem=tap_send.at[step], recv_sem=tap_recv.at[step],
            device_id=(target, col), device_id_type=MESH,
        )
        copy.start()
        tap_copies.append(copy)
    for part in range(parts):
        for step in range(1, blocks):
            target = lax.rem(me + step, blocks)
            copy = pltpu.make_async_remote_copy(
                src_ref=pieces.at[lax.rem(target + near, blocks), part], dst_ref=rows.at[part, me],
                send_sem=in_send.at[part, step], recv_sem=in_recv.at[part, step],
                device_id=(target, col), device_id_type=MESH,
            )
            copy.start()
            in_copies[part].append(copy)
        for step in range(1, near if part == 0 else 1):
            target = base + lax.rem(me + step, near)
            copy = pltpu.make_async_remote_copy(
                src_ref=pieces.at[target], dst_ref=side.at[local],
                send_sem=side_send.at[step], recv_sem=side_recv.at[step],
                device_id=(target, col), device_id_type=MESH,
            )
            copy.start()
            side_copies.append(copy)
    side[local] = pieces[me]
    filt[me, col] = tap_pieces[lax.rem(me, count)]
    for part in range(parts):
        rows[part, me] = pieces[lax.rem(me + near, blocks), part]

    for copy in tap_copies:
        copy.wait_recv()
    for step in range(1, groups):
        copy = pltpu.make_async_remote_copy(
            src_ref=filt.at[:, col], dst_ref=filt.at[:, col],
            send_sem=slab_send.at[step], recv_sem=slab_recv.at[step],
            device_id=(me, lax.rem(col + step, groups)), device_id_type=MESH,
        )
        copy.start()
        slab_copies.append(copy)

    for load in loads[5:]:
        load.wait()
    first_all[...] = stack_left(first_ref[...])
    last_all[...] = stack_left(last_ref[...])
    mid_all[...] = stack_right(mid_ref[...])
    inv_all[...] = stack_right(inv_ref[...])
    shift_re, shift_im = shift_ref[0:1, :], shift_ref[1:2, :]

    def twisted(mixed, part):
        cut = slice(part * LANES, (part + 1) * LANES)
        real, imag = mixed[:SIDE], mixed[SIDE:]
        turn_re, turn_im = turn_re_ref[:, cut], turn_im_ref[:, cut]
        return real * turn_re - imag * turn_im, real * turn_im + imag * turn_re

    def spectrum(near_part, far_part):
        (near_re, near_im), (far_re, far_im) = near_part, far_part
        gap_re, gap_im = near_re - far_re, near_im - far_im
        even = jnp.concatenate([near_re + far_re, near_im + far_im], axis=1)
        odd = jnp.concatenate(
            [gap_re * shift_re - gap_im * shift_im, gap_re * shift_im + gap_im * shift_re], axis=1
        )
        total = mul(stack_left(jnp.concatenate([even, odd], axis=0)), mid_all[...])
        return total[:, :LANES], total[:, LANES:]

    def levels(row_re, row_im, tap_re, tap_im):
        joined = jnp.concatenate(
            [row_re * tap_re - row_im * tap_im, row_re * tap_im + row_im * tap_re], axis=1
        )
        coarse = mul(stack_left(joined), inv_all[...])
        even_re, even_im = coarse[:SIDE, :LANES], coarse[:SIDE, LANES:]
        odd_re, odd_im = coarse[SIDE:, :LANES], coarse[SIDE:, LANES:]
        gap_re = odd_re * shift_re + odd_im * shift_im
        gap_im = odd_im * shift_re - odd_re * shift_im
        found = []
        for part, real, imag in ((0, even_re + gap_re, even_im + gap_im), (1, even_re - gap_re, even_im - gap_im)):
            cut = slice(part * LANES, (part + 1) * LANES)
            turn_re, turn_im = turn_re_ref[:, cut], turn_im_ref[:, cut]
            found.append(jnp.concatenate(
                [real * turn_re + imag * turn_im, imag * turn_re - real * turn_im], axis=0
            ))
        return found

    def row_part(part):
        for copy in in_copies[part]:
            copy.wait_recv()
        return twisted(mul(first_all[...], stack_right(rows[part].reshape(SIDE, LANES))), part)

    row_near = row_part(0)
    for copy in slab_copies:
        copy.wait_recv()
    taps = jnp.concatenate([filt[:, :, part].reshape(SIDE, LANES) for part in range(parts)], axis=1)
    mixed = mul(first_all[...], stack_right(taps))
    tap_re, tap_im = spectrum(twisted(mixed[:, :LANES], 0), twisted(mixed[:, LANES:], 1))
    tap_im = tap_im * jnp.where(me < near, -1.0, 1.0)

    for copy in side_copies:
        copy.wait_recv()
    tokens = jnp.concatenate([side[:, part].reshape(depth, LANES) for part in range(parts)], axis=1)
    held = jnp.concatenate([first_all[:, third * SIDE:third * SIDE + depth] for third in range(3)], axis=1)
    mixed = mul(held, stack_right(tokens))
    side_re, side_im = spectrum(twisted(mixed[:, :LANES], 0), twisted(mixed[:, LANES:], 1))
    level = jnp.concatenate(levels(side_re, side_im, tap_re, -tap_im), axis=1)
    rebuilt = mul(last_all[:depth], stack_right(level))
    for part in range(parts):
        side_result[:, part] = rebuilt[:, part * LANES:(part + 1) * LANES].reshape(near, *side_result.shape[2:])
    for step in range(1, near):
        target = lax.rem(me + step, near)
        copy = pltpu.make_async_remote_copy(
            src_ref=side_result.at[target], dst_ref=back.at[me],
            send_sem=home_send.at[step], recv_sem=home_recv.at[step],
            device_id=(base + target, col), device_id_type=MESH,
        )
        copy.start()
        home_copies.append(copy)
    back[me] = side_result[local]

    row_re, row_im = spectrum(row_near, row_part(1))
    kept = pl.ds(pl.multiple_of((me // near) * depth, depth), depth)
    place = lax.rem(me + near, blocks)
    for part, level in enumerate(levels(row_re, row_im, tap_re, tap_im)):
        result[part] = mul(last_all[kept, :], stack_right(level)).reshape(result.shape[1:])
        for step in range(1, near):
            target = lax.rem(me + step, near)
            copy = pltpu.make_async_remote_copy(
                src_ref=result.at[part, target], dst_ref=back.at[place, part],
                send_sem=out_send.at[part, step], recv_sem=out_recv.at[part, step],
                device_id=(base + target, col), device_id_type=MESH,
            )
            copy.start()
            out_copies[part].append(copy)
        back[place, part] = result[part, local]
    for copy in home_copies:
        copy.wait_recv()
    for part in range(parts):
        for copy in out_copies[part]:
            copy.wait_recv()
        for row in range(back.shape[2]):
            out_ref[:, span(row, part)] = back[:, part, row, :]
    for copy in tap_copies + sum(in_copies, []) + slab_copies + side_copies + home_copies + sum(out_copies, []):
        copy.wait_send()


def rows_on_device(query_gate, key_gate, value_input, filter_taps, cotangent):
    count, width = query_gate.shape
    blocks = lax.axis_size("seq")
    groups = lax.axis_size("chan")
    high = width // SIDE
    near = blocks // 2
    parts = SIDE // LANES
    tables = fourier_tables()
    f32, bf16 = jnp.float32, jnp.bfloat16
    operands = (key_gate, value_input, query_gate, cotangent, filter_taps, *[jnp.asarray(table) for table in tables])
    sums = pl.pallas_call(
        partial(row_kernel, blocks, groups),
        out_shape=jax.ShapeDtypeStruct((blocks, width), f32),
        in_specs=[pl.BlockSpec(memory_space=pl.ANY)] * len(operands),
        out_specs=pl.BlockSpec(memory_space=pltpu.VMEM),
        scratch_shapes=[
            *[pltpu.VMEM(operand.shape, f32) for operand in operands],
            pltpu.VMEM((blocks, parts, high, LANES), f32),
            pltpu.VMEM((count, parts, high // groups, LANES), f32),
            pltpu.VMEM((parts, blocks, high, LANES), f32),
            pltpu.VMEM((near, parts, high, LANES), f32),
            pltpu.VMEM((blocks, groups, parts, high // groups, LANES), f32),
            pltpu.VMEM((parts, near, high, LANES), f32),
            pltpu.VMEM((near, parts, high, LANES), f32),
            pltpu.VMEM((blocks, parts, high, LANES), f32),
            pltpu.VMEM((2 * SIDE, 3 * SIDE), bf16),
            pltpu.VMEM((3 * SIDE, SIDE), bf16),
            pltpu.VMEM((3 * SIDE, SIDE), bf16),
            pltpu.VMEM((SIDE, 6 * SIDE), bf16),
            pltpu.SemaphoreType.DMA((len(operands),)),
            pltpu.SemaphoreType.DMA((blocks,)),
            pltpu.SemaphoreType.DMA((blocks,)),
            pltpu.SemaphoreType.DMA((groups,)),
            pltpu.SemaphoreType.DMA((groups,)),
            pltpu.SemaphoreType.DMA((parts, blocks)),
            pltpu.SemaphoreType.DMA((parts, blocks)),
            pltpu.SemaphoreType.DMA((parts, blocks)),
            pltpu.SemaphoreType.DMA((parts, blocks)),
            *[pltpu.SemaphoreType.DMA((near,))] * 4,
        ],
        compiler_params=pltpu.CompilerParams(
            collective_id=0, has_side_effects=True, vmem_limit_bytes=VMEM_BYTES
        ),
    )(*operands)
    convolved, gated_grad = sums[:count], sums[count:]
    return (cotangent * convolved, gated_grad * value_input, gated_grad * key_gate)


def one_row_each(query_gate, filter_taps):
    count, width = query_gate.shape
    blocks = lax.axis_size("seq")
    groups = lax.axis_size("chan")
    return (
        blocks == 2 * count
        and filter_taps.shape[0] == count
        and blocks * width == SIDE * SIDE
        and width % (8 * groups * SIDE) == 0
    )


def phase_table(row_count, column_count, offset, period, direction):
    row_index = lax.broadcasted_iota(jnp.int32, (row_count, column_count), 0)
    column_index = lax.broadcasted_iota(jnp.int32, (row_count, column_count), 1)
    phases = row_index * (column_index + offset) % period
    angles = phases.astype(jnp.float32) * (direction * 2.0 * math.pi / period)
    return (jnp.cos(angles), jnp.sin(angles))


def complex_mix(formula, table_real, table_imag, data_real, data_imag):
    product = partial(jnp.einsum, formula, precision=lax.Precision.HIGHEST)
    return (
        product(table_real, data_real) - product(table_imag, data_imag),
        product(table_real, data_imag) + product(table_imag, data_real),
    )


def regroup_tokens(signal):
    return lax.all_to_all(signal, "seq", split_axis=1, concat_axis=1, tiled=True)


def regroup_spectrum(part_real, part_imag):
    return (
        lax.all_to_all(part_real, "seq", split_axis=1, concat_axis=1, tiled=True),
        lax.all_to_all(part_imag, "seq", split_axis=1, concat_axis=1, tiled=True),
    )


def finish_forward(moved_real, moved_imag, blocks, width, tokens):
    outer_real, outer_imag = phase_table(blocks, blocks, 0, blocks, -1.0)
    coarse_real, coarse_imag = complex_mix(
        "ur,crjq->cujq", outer_real, outer_imag, moved_real, moved_imag
    )
    shift_real, shift_imag = phase_table(blocks, width, 0, tokens, -1.0)
    shift_real = shift_real[None, :, None, :]
    shift_imag = shift_imag[None, :, None, :]
    twisted_real = coarse_real * shift_real - coarse_imag * shift_imag
    twisted_imag = coarse_real * shift_imag + coarse_imag * shift_real
    inner_real, inner_imag = phase_table(width, width, 0, width, -1.0)
    return complex_mix("qv,cujq->cujv", inner_real, inner_imag, twisted_real, twisted_imag)


def start_inverse(spectrum_real, spectrum_imag, blocks, width, tokens):
    inner_real, inner_imag = phase_table(width, width, 0, width, 1.0)
    fine_real, fine_imag = complex_mix(
        "vq,cujv->cujq", inner_real, inner_imag, spectrum_real, spectrum_imag
    )
    shift_real, shift_imag = phase_table(blocks, width, 0, tokens, 1.0)
    shift_real = shift_real[None, :, None, :]
    shift_imag = shift_imag[None, :, None, :]
    untwisted_real = fine_real * shift_real - fine_imag * shift_imag
    untwisted_imag = fine_real * shift_imag + fine_imag * shift_real
    outer_real, outer_imag = phase_table(blocks, blocks, 0, blocks, 1.0)
    return complex_mix("ru,cujq->crjq", outer_real, outer_imag, untwisted_real, untwisted_imag)


def forward_spectrum(signal):
    count, tokens = signal.shape
    blocks = lax.axis_size("seq")
    width = tokens // blocks
    freqs = 2 * blocks
    period = freqs * tokens
    rank = lax.axis_index("seq")
    gathered = regroup_tokens(signal.reshape(count, blocks, width))
    product = partial(jnp.einsum, "kp,cpq->ckq", precision=lax.Precision.HIGHEST)
    anchor = rank * width
    first_real, first_imag = phase_table(freqs, blocks, 0, freqs, -1.0)
    mixed_real = product(first_real, gathered)
    mixed_imag = product(first_imag, gathered)
    turn_real, turn_imag = phase_table(freqs, width, anchor, period, -1.0)
    moved_real, moved_imag = regroup_spectrum(
        mixed_real * turn_real - mixed_imag * turn_imag,
        mixed_real * turn_imag + mixed_imag * turn_real,
    )
    moved_real = moved_real.reshape(count, blocks, 2, width)
    moved_imag = moved_imag.reshape(count, blocks, 2, width)
    return finish_forward(moved_real, moved_imag, blocks, width, tokens)


def inverse_spectrum(spectrum_real, spectrum_imag):
    count, blocks, per_device, width = spectrum_real.shape
    tokens = blocks * width
    freqs = 2 * blocks
    period = freqs * tokens
    rank = lax.axis_index("seq")
    spread_real, spread_imag = start_inverse(spectrum_real, spectrum_imag, blocks, width, tokens)
    product = partial(jnp.einsum, "kp,ckq->cpq", precision=lax.Precision.HIGHEST)
    anchor = rank * width
    moved_real, moved_imag = regroup_spectrum(
        spread_real.reshape(count, blocks * per_device, width),
        spread_imag.reshape(count, blocks * per_device, width),
    )
    turn_real, turn_imag = phase_table(freqs, width, anchor, period, 1.0)
    level_real = moved_real * turn_real - moved_imag * turn_imag
    level_imag = moved_real * turn_imag + moved_imag * turn_real
    first_real, first_imag = phase_table(freqs, blocks, 0, freqs, 1.0)
    rebuilt = (product(first_real, level_real) - product(first_imag, level_imag)) * (1.0 / period)
    return regroup_tokens(rebuilt).reshape(count, tokens)


def on_device(query_gate, key_gate, value_input, filter_taps, cotangent):
    if one_row_each(query_gate, filter_taps):
        return rows_on_device(query_gate, key_gate, value_input, filter_taps, cotangent)
    block_taps = lax.all_gather(filter_taps, "chan", axis=1, tiled=True)
    filter_real, filter_imag = forward_spectrum(block_taps)
    gated = key_gate * value_input
    weighted = cotangent * query_gate
    gated_real, gated_imag = forward_spectrum(gated)
    convolved = inverse_spectrum(
        gated_real * filter_real - gated_imag * filter_imag,
        gated_real * filter_imag + gated_imag * filter_real,
    )
    weighted_real, weighted_imag = forward_spectrum(weighted)
    gated_grad = inverse_spectrum(
        weighted_real * filter_real + weighted_imag * filter_imag,
        weighted_imag * filter_real - weighted_real * filter_imag,
    )
    return (cotangent * convolved, gated_grad * value_input, gated_grad * key_gate)


def solution(mesh):
    in_specs = (
        P("chan", "seq"),
        P("chan", "seq"),
        P("chan", "seq"),
        P(None, ("seq", "chan")),
        P("chan", "seq"),
    )
    out_specs = (P("chan", "seq"), P("chan", "seq"), P("chan", "seq"))
    return jax.shard_map(
        on_device, mesh=mesh, in_specs=in_specs, out_specs=out_specs, check_vma=False
    )
```

```python
from functools import partial
import math

import jax
import jax.numpy as jnp
import numpy as np
from jax import lax
from jax.experimental import pallas as pl
from jax.experimental.pallas import tpu as pltpu
from jax.sharding import PartitionSpec as P

MESH = pl.DeviceIdType.MESH
SIDE = 256
LANES = 128
VMEM_BYTES = 63 * 1024 * 1024


def fourier_tables():
    total = SIDE * SIDE
    index = np.arange(SIDE, dtype=np.float64)
    outer = 2.0 * np.pi * np.outer(index + 0.25, index) / SIDE
    first = np.concatenate([np.cos(outer), -np.sin(outer)], axis=0)
    last = first.T / total
    inner_index = np.arange(LANES, dtype=np.float64)
    inner = 2.0 * np.pi * (np.outer(inner_index, inner_index) % LANES) / LANES
    cosine, sine = np.cos(inner), np.sin(inner)
    middle = np.block([[cosine, -sine], [sine, cosine]])
    inverse = np.block([[cosine, sine], [-sine, cosine]])
    twist = 2.0 * np.pi * np.outer(index + 0.25, index) / total
    odd = 2.0 * np.pi * inner_index / SIDE
    shift = np.stack([np.cos(odd), -np.sin(odd)] * 4)
    tables = (first, middle, inverse, last, np.cos(twist), -np.sin(twist), shift)
    return tuple(table.astype(np.float32) for table in tables)


def split(value):
    high = value.astype(jnp.bfloat16)
    low = (value - high.astype(jnp.float32)).astype(jnp.bfloat16)
    return high, low


def stack_left(value, axis=1):
    high, low = split(value)
    return jnp.concatenate([high, high, low], axis=axis)


def stack_right(value, axis=0):
    high, low = split(value)
    return jnp.concatenate([high, low, high], axis=axis)


def mul(left, right):
    return jnp.dot(left, right, preferred_element_type=jnp.float32)


def row_kernel(
    blocks, groups, k_hbm, v_hbm, q_hbm, c_hbm, taps_hbm,
    first_hbm, mid_hbm, inv_hbm, last_hbm, turn_re_hbm, turn_im_hbm, shift_hbm, out_ref,
    k_ref, v_ref, q_ref, c_ref, taps_ref, first_ref, mid_ref, inv_ref, last_ref, turn_re_ref, turn_im_ref, shift_ref,
    pieces, tap_pieces, rows, side, filt, result, side_result, back,
    first_all, mid_all, inv_all, last_all,
    load_sem, tap_send, tap_recv, slab_send, slab_recv, in_send, in_recv, out_send, out_recv,
    side_send, side_recv, home_send, home_recv,
):
    me = lax.axis_index("seq")
    col = lax.axis_index("chan")
    count = k_ref.shape[0]
    parts = SIDE // LANES
    near = blocks // 2
    base = (me // near) * near
    local = lax.rem(me, near)
    depth = SIDE // 2

    sources = (taps_hbm, k_hbm, v_hbm, c_hbm, q_hbm, first_hbm, mid_hbm, inv_hbm, turn_re_hbm, turn_im_hbm, last_hbm, shift_hbm)
    targets = (taps_ref, k_ref, v_ref, c_ref, q_ref, first_ref, mid_ref, inv_ref, turn_re_ref, turn_im_ref, last_ref, shift_ref)
    loads = [
        pltpu.make_async_copy(source, target, load_sem.at[place])
        for place, (source, target) in enumerate(zip(sources, targets))
    ]
    for load in loads:
        load.start()

    barrier = pltpu.get_barrier_semaphore()
    for step in range(1, blocks):
        pl.semaphore_signal(barrier, inc=1, device_id=(lax.rem(me + step, blocks), col), device_id_type=MESH)
    for step in range(1, groups):
        pl.semaphore_signal(barrier, inc=1, device_id=(me, lax.rem(col + step, groups)), device_id_type=MESH)

    def span(row, part):
        return slice(row * SIDE + part * LANES, row * SIDE + (part + 1) * LANES)

    loads[0].wait()
    for part in range(parts):
        for row in range(taps_ref.shape[1] // SIDE):
            tap_pieces[:, part, row, :] = taps_ref[:, span(row, part)]
    tap_copies, slab_copies, side_copies, home_copies = [], [], [], []
    in_copies, out_copies = [[] for _ in range(parts)], [[] for _ in range(parts)]
    pl.semaphore_wait(barrier, blocks + groups - 2)
    for step in range(1, blocks):
        target = lax.rem(me + step, blocks)
        copy = pltpu.make_async_remote_copy(
            src_ref=tap_pieces.at[lax.rem(target, count)], dst_ref=filt.at[me, col],
            send_sem=tap_send.at[step], recv_sem=tap_recv.at[step],
            device_id=(target, col), device_id_type=MESH,
        )
        copy.start()
        tap_copies.append(copy)

    for load in loads[1:5]:
        load.wait()
    for part in range(parts):
        for row in range(k_ref.shape[1] // SIDE):
            tokens = span(row, part)
            pieces[:count, part, row, :] = k_ref[:, tokens] * v_ref[:, tokens]
            pieces[count:, part, row, :] = c_ref[:, tokens] * q_ref[:, tokens]
        for step in range(1, near if part == parts - 1 else 1):
            target = base + lax.rem(me + step, near)
            copy = pltpu.make_async_remote_copy(
                src_ref=pieces.at[target], dst_ref=side.at[local],
                send_sem=side_send.at[step], recv_sem=side_recv.at[step],
                device_id=(target, col), device_id_type=MESH,
            )
            copy.start()
            side_copies.append(copy)
        for step in range(1, blocks):
            target = lax.rem(me + step, blocks)
            copy = pltpu.make_async_remote_copy(
                src_ref=pieces.at[lax.rem(target + near, blocks), part], dst_ref=rows.at[part, me],
                send_sem=in_send.at[part, step], recv_sem=in_recv.at[part, step],
                device_id=(target, col), device_id_type=MESH,
            )
            copy.start()
            in_copies[part].append(copy)
    side[local] = pieces[me]
    filt[me, col] = tap_pieces[lax.rem(me, count)]
    for part in range(parts):
        rows[part, me] = pieces[lax.rem(me + near, blocks), part]

    for copy in tap_copies:
        copy.wait_recv()
    for step in range(1, groups):
        copy = pltpu.make_async_remote_copy(
            src_ref=filt.at[:, col], dst_ref=filt.at[:, col],
            send_sem=slab_send.at[step], recv_sem=slab_recv.at[step],
            device_id=(me, lax.rem(col + step, groups)), device_id_type=MESH,
        )
        copy.start()
        slab_copies.append(copy)

    for load in loads[5:]:
        load.wait()
    first_all[...] = stack_left(first_ref[...])
    last_all[...] = stack_left(last_ref[...])
    mid_all[...] = stack_right(mid_ref[...])
    inv_all[...] = stack_right(inv_ref[...])
    shift_re, shift_im = shift_ref[0:1, :], shift_ref[1:2, :]

    def twisted(mixed, part):
        cut = slice(part * LANES, (part + 1) * LANES)
        real, imag = mixed[:SIDE], mixed[SIDE:]
        turn_re, turn_im = turn_re_ref[:, cut], turn_im_ref[:, cut]
        return real * turn_re - imag * turn_im, real * turn_im + imag * turn_re

    def spectrum(near_part, far_part):
        (near_re, near_im), (far_re, far_im) = near_part, far_part
        gap_re, gap_im = near_re - far_re, near_im - far_im
        even = jnp.concatenate([near_re + far_re, near_im + far_im], axis=1)
        odd = jnp.concatenate(
            [gap_re * shift_re - gap_im * shift_im, gap_re * shift_im + gap_im * shift_re], axis=1
        )
        total = mul(stack_left(jnp.concatenate([even, odd], axis=0)), mid_all[...])
        return total[:, :LANES], total[:, LANES:]

    def levels(row_re, row_im, tap_re, tap_im):
        joined = jnp.concatenate(
            [row_re * tap_re - row_im * tap_im, row_re * tap_im + row_im * tap_re], axis=1
        )
        coarse = mul(stack_left(joined), inv_all[...])
        even_re, even_im = coarse[:SIDE, :LANES], coarse[:SIDE, LANES:]
        odd_re, odd_im = coarse[SIDE:, :LANES], coarse[SIDE:, LANES:]
        gap_re = odd_re * shift_re + odd_im * shift_im
        gap_im = odd_im * shift_re - odd_re * shift_im
        found = []
        for part, real, imag in ((0, even_re + gap_re, even_im + gap_im), (1, even_re - gap_re, even_im - gap_im)):
            cut = slice(part * LANES, (part + 1) * LANES)
            turn_re, turn_im = turn_re_ref[:, cut], turn_im_ref[:, cut]
            found.append(jnp.concatenate(
                [real * turn_re + imag * turn_im, imag * turn_re - real * turn_im], axis=0
            ))
        return found

    def row_part(part):
        for copy in in_copies[part]:
            copy.wait_recv()
        return twisted(mul(first_all[...], stack_right(rows[part].reshape(SIDE, LANES))), part)

    row_near = row_part(0)
    for copy in side_copies:
        copy.wait_recv()
    tokens = jnp.concatenate([side[:, part].reshape(depth, LANES) for part in range(parts)], axis=1)
    held = jnp.concatenate([first_all[:, third * SIDE:third * SIDE + depth] for third in range(3)], axis=1)
    mixed = mul(held, stack_right(tokens))
    side_re, side_im = spectrum(twisted(mixed[:, :LANES], 0), twisted(mixed[:, LANES:], 1))
    for copy in slab_copies:
        copy.wait_recv()
    taps = jnp.concatenate([filt[:, :, part].reshape(SIDE, LANES) for part in range(parts)], axis=1)
    mixed = mul(first_all[...], stack_right(taps))
    tap_re, tap_im = spectrum(twisted(mixed[:, :LANES], 0), twisted(mixed[:, LANES:], 1))
    tap_im = tap_im * jnp.where(me < near, -1.0, 1.0)

    level = jnp.concatenate(levels(side_re, side_im, tap_re, -tap_im), axis=1)
    rebuilt = mul(last_all[:depth], stack_right(level))
    for part in range(parts):
        side_result[:, part] = rebuilt[:, part * LANES:(part + 1) * LANES].reshape(near, *side_result.shape[2:])
    for step in range(1, near):
        target = lax.rem(me + step, near)
        copy = pltpu.make_async_remote_copy(
            src_ref=side_result.at[target], dst_ref=back.at[me],
            send_sem=home_send.at[step], recv_sem=home_recv.at[step],
            device_id=(base + target, col), device_id_type=MESH,
        )
        copy.start()
        home_copies.append(copy)
    back[me] = side_result[local]

    row_re, row_im = spectrum(row_near, row_part(1))
    kept = pl.ds(pl.multiple_of((me // near) * depth, depth), depth)
    place = lax.rem(me + near, blocks)
    for part, level in enumerate(levels(row_re, row_im, tap_re, tap_im)):
        result[part] = mul(last_all[kept, :], stack_right(level)).reshape(result.shape[1:])
        for step in range(1, near):
            target = lax.rem(me + step, near)
            copy = pltpu.make_async_remote_copy(
                src_ref=result.at[part, target], dst_ref=back.at[place, part],
                send_sem=out_send.at[part, step], recv_sem=out_recv.at[part, step],
                device_id=(base + target, col), device_id_type=MESH,
            )
            copy.start()
            out_copies[part].append(copy)
        back[place, part] = result[part, local]
    for copy in home_copies:
        copy.wait_recv()
    for part in range(parts):
        for copy in out_copies[part]:
            copy.wait_recv()
        for row in range(back.shape[2]):
            out_ref[:, span(row, part)] = back[:, part, row, :]
    for copy in tap_copies + sum(in_copies, []) + slab_copies + side_copies + home_copies + sum(out_copies, []):
        copy.wait_send()


def rows_on_device(query_gate, key_gate, value_input, filter_taps, cotangent):
    count, width = query_gate.shape
    blocks = lax.axis_size("seq")
    groups = lax.axis_size("chan")
    high = width // SIDE
    near = blocks // 2
    parts = SIDE // LANES
    tables = fourier_tables()
    f32, bf16 = jnp.float32, jnp.bfloat16
    operands = (key_gate, value_input, query_gate, cotangent, filter_taps, *[jnp.asarray(table) for table in tables])
    sums = pl.pallas_call(
        partial(row_kernel, blocks, groups),
        out_shape=jax.ShapeDtypeStruct((blocks, width), f32),
        in_specs=[pl.BlockSpec(memory_space=pl.ANY)] * len(operands),
        out_specs=pl.BlockSpec(memory_space=pltpu.VMEM),
        scratch_shapes=[
            *[pltpu.VMEM(operand.shape, f32) for operand in operands],
            pltpu.VMEM((blocks, parts, high, LANES), f32),
            pltpu.VMEM((count, parts, high // groups, LANES), f32),
            pltpu.VMEM((parts, blocks, high, LANES), f32),
            pltpu.VMEM((near, parts, high, LANES), f32),
            pltpu.VMEM((blocks, groups, parts, high // groups, LANES), f32),
            pltpu.VMEM((parts, near, high, LANES), f32),
            pltpu.VMEM((near, parts, high, LANES), f32),
            pltpu.VMEM((blocks, parts, high, LANES), f32),
            pltpu.VMEM((2 * SIDE, 3 * SIDE), bf16),
            pltpu.VMEM((3 * SIDE, SIDE), bf16),
            pltpu.VMEM((3 * SIDE, SIDE), bf16),
            pltpu.VMEM((SIDE, 6 * SIDE), bf16),
            pltpu.SemaphoreType.DMA((len(operands),)),
            pltpu.SemaphoreType.DMA((blocks,)),
            pltpu.SemaphoreType.DMA((blocks,)),
            pltpu.SemaphoreType.DMA((groups,)),
            pltpu.SemaphoreType.DMA((groups,)),
            pltpu.SemaphoreType.DMA((parts, blocks)),
            pltpu.SemaphoreType.DMA((parts, blocks)),
            pltpu.SemaphoreType.DMA((parts, blocks)),
            pltpu.SemaphoreType.DMA((parts, blocks)),
            *[pltpu.SemaphoreType.DMA((near,))] * 4,
        ],
        compiler_params=pltpu.CompilerParams(
            collective_id=0, has_side_effects=True, vmem_limit_bytes=VMEM_BYTES
        ),
    )(*operands)
    convolved, gated_grad = sums[:count], sums[count:]
    return (cotangent * convolved, gated_grad * value_input, gated_grad * key_gate)


def one_row_each(query_gate, filter_taps):
    count, width = query_gate.shape
    blocks = lax.axis_size("seq")
    groups = lax.axis_size("chan")
    return (
        blocks == 2 * count
        and filter_taps.shape[0] == count
        and blocks * width == SIDE * SIDE
        and width % (8 * groups * SIDE) == 0
    )


def phase_table(row_count, column_count, offset, period, direction):
    row_index = lax.broadcasted_iota(jnp.int32, (row_count, column_count), 0)
    column_index = lax.broadcasted_iota(jnp.int32, (row_count, column_count), 1)
    phases = row_index * (column_index + offset) % period
    angles = phases.astype(jnp.float32) * (direction * 2.0 * math.pi / period)
    return (jnp.cos(angles), jnp.sin(angles))


def complex_mix(formula, table_real, table_imag, data_real, data_imag):
    product = partial(jnp.einsum, formula, precision=lax.Precision.HIGHEST)
    return (
        product(table_real, data_real) - product(table_imag, data_imag),
        product(table_real, data_imag) + product(table_imag, data_real),
    )


def regroup_tokens(signal):
    return lax.all_to_all(signal, "seq", split_axis=1, concat_axis=1, tiled=True)


def regroup_spectrum(part_real, part_imag):
    return (
        lax.all_to_all(part_real, "seq", split_axis=1, concat_axis=1, tiled=True),
        lax.all_to_all(part_imag, "seq", split_axis=1, concat_axis=1, tiled=True),
    )


def finish_forward(moved_real, moved_imag, blocks, width, tokens):
    outer_real, outer_imag = phase_table(blocks, blocks, 0, blocks, -1.0)
    coarse_real, coarse_imag = complex_mix(
        "ur,crjq->cujq", outer_real, outer_imag, moved_real, moved_imag
    )
    shift_real, shift_imag = phase_table(blocks, width, 0, tokens, -1.0)
    shift_real = shift_real[None, :, None, :]
    shift_imag = shift_imag[None, :, None, :]
    twisted_real = coarse_real * shift_real - coarse_imag * shift_imag
    twisted_imag = coarse_real * shift_imag + coarse_imag * shift_real
    inner_real, inner_imag = phase_table(width, width, 0, width, -1.0)
    return complex_mix("qv,cujq->cujv", inner_real, inner_imag, twisted_real, twisted_imag)


def start_inverse(spectrum_real, spectrum_imag, blocks, width, tokens):
    inner_real, inner_imag = phase_table(width, width, 0, width, 1.0)
    fine_real, fine_imag = complex_mix(
        "vq,cujv->cujq", inner_real, inner_imag, spectrum_real, spectrum_imag
    )
    shift_real, shift_imag = phase_table(blocks, width, 0, tokens, 1.0)
    shift_real = shift_real[None, :, None, :]
    shift_imag = shift_imag[None, :, None, :]
    untwisted_real = fine_real * shift_real - fine_imag * shift_imag
    untwisted_imag = fine_real * shift_imag + fine_imag * shift_real
    outer_real, outer_imag = phase_table(blocks, blocks, 0, blocks, 1.0)
    return complex_mix("ru,cujq->crjq", outer_real, outer_imag, untwisted_real, untwisted_imag)


def forward_spectrum(signal):
    count, tokens = signal.shape
    blocks = lax.axis_size("seq")
    width = tokens // blocks
    freqs = 2 * blocks
    period = freqs * tokens
    rank = lax.axis_index("seq")
    gathered = regroup_tokens(signal.reshape(count, blocks, width))
    product = partial(jnp.einsum, "kp,cpq->ckq", precision=lax.Precision.HIGHEST)
    anchor = rank * width
    first_real, first_imag = phase_table(freqs, blocks, 0, freqs, -1.0)
    mixed_real = product(first_real, gathered)
    mixed_imag = product(first_imag, gathered)
    turn_real, turn_imag = phase_table(freqs, width, anchor, period, -1.0)
    moved_real, moved_imag = regroup_spectrum(
        mixed_real * turn_real - mixed_imag * turn_imag,
        mixed_real * turn_imag + mixed_imag * turn_real,
    )
    moved_real = moved_real.reshape(count, blocks, 2, width)
    moved_imag = moved_imag.reshape(count, blocks, 2, width)
    return finish_forward(moved_real, moved_imag, blocks, width, tokens)


def inverse_spectrum(spectrum_real, spectrum_imag):
    count, blocks, per_device, width = spectrum_real.shape
    tokens = blocks * width
    freqs = 2 * blocks
    period = freqs * tokens
    rank = lax.axis_index("seq")
    spread_real, spread_imag = start_inverse(spectrum_real, spectrum_imag, blocks, width, tokens)
    product = partial(jnp.einsum, "kp,ckq->cpq", precision=lax.Precision.HIGHEST)
    anchor = rank * width
    moved_real, moved_imag = regroup_spectrum(
        spread_real.reshape(count, blocks * per_device, width),
        spread_imag.reshape(count, blocks * per_device, width),
    )
    turn_real, turn_imag = phase_table(freqs, width, anchor, period, 1.0)
    level_real = moved_real * turn_real - moved_imag * turn_imag
    level_imag = moved_real * turn_imag + moved_imag * turn_real
    first_real, first_imag = phase_table(freqs, blocks, 0, freqs, 1.0)
    rebuilt = (product(first_real, level_real) - product(first_imag, level_imag)) * (1.0 / period)
    return regroup_tokens(rebuilt).reshape(count, tokens)


def on_device(query_gate, key_gate, value_input, filter_taps, cotangent):
    if one_row_each(query_gate, filter_taps):
        return rows_on_device(query_gate, key_gate, value_input, filter_taps, cotangent)
    block_taps = lax.all_gather(filter_taps, "chan", axis=1, tiled=True)
    filter_real, filter_imag = forward_spectrum(block_taps)
    gated = key_gate * value_input
    weighted = cotangent * query_gate
    gated_real, gated_imag = forward_spectrum(gated)
    convolved = inverse_spectrum(
        gated_real * filter_real - gated_imag * filter_imag,
        gated_real * filter_imag + gated_imag * filter_real,
    )
    weighted_real, weighted_imag = forward_spectrum(weighted)
    gated_grad = inverse_spectrum(
        weighted_real * filter_real + weighted_imag * filter_imag,
        weighted_imag * filter_real - weighted_real * filter_imag,
    )
    return (cotangent * convolved, gated_grad * value_input, gated_grad * key_gate)


def solution(mesh):
    in_specs = (
        P("chan", "seq"),
        P("chan", "seq"),
        P("chan", "seq"),
        P(None, ("seq", "chan")),
        P("chan", "seq"),
    )
    out_specs = (P("chan", "seq"), P("chan", "seq"), P("chan", "seq"))
    return jax.shard_map(
        on_device, mesh=mesh, in_specs=in_specs, out_specs=out_specs, check_vma=False
    )
```

```python
from functools import partial
import math

import jax
import jax.numpy as jnp
import numpy as np
from jax import lax
from jax.experimental import pallas as pl
from jax.experimental.pallas import tpu as pltpu
from jax.sharding import PartitionSpec as P

MESH = pl.DeviceIdType.MESH
SIDE = 256
LANES = 128
VMEM_BYTES = 63 * 1024 * 1024


def fourier_tables():
    total = SIDE * SIDE
    index = np.arange(SIDE, dtype=np.float64)
    outer = 2.0 * np.pi * np.outer(index + 0.25, index) / SIDE
    first = np.concatenate([np.cos(outer), -np.sin(outer)], axis=0)
    last = first.T / total
    inner_index = np.arange(LANES, dtype=np.float64)
    inner = 2.0 * np.pi * (np.outer(inner_index, inner_index) % LANES) / LANES
    cosine, sine = np.cos(inner), np.sin(inner)
    middle = np.block([[cosine, -sine], [sine, cosine]])
    inverse = np.block([[cosine, sine], [-sine, cosine]])
    twist = 2.0 * np.pi * np.outer(index + 0.25, index) / total
    odd = 2.0 * np.pi * inner_index / SIDE
    shift = np.stack([np.cos(odd), -np.sin(odd)] * 4)
    tables = (first, middle, inverse, last, np.cos(twist), -np.sin(twist), shift)
    return tuple(table.astype(np.float32) for table in tables)


def split(value):
    high = value.astype(jnp.bfloat16)
    low = (value - high.astype(jnp.float32)).astype(jnp.bfloat16)
    return high, low


def stack_left(value, axis=1):
    high, low = split(value)
    return jnp.concatenate([high, high, low], axis=axis)


def stack_right(value, axis=0):
    high, low = split(value)
    return jnp.concatenate([high, low, high], axis=axis)


def mul(left, right):
    return jnp.dot(left, right, preferred_element_type=jnp.float32)


def row_kernel(
    blocks, groups, k_hbm, v_hbm, q_hbm, c_hbm, taps_hbm,
    first_hbm, mid_hbm, inv_hbm, last_hbm, turn_re_hbm, turn_im_hbm, shift_hbm, out_ref,
    k_ref, v_ref, q_ref, c_ref, taps_ref, first_ref, mid_ref, inv_ref, last_ref, turn_re_ref, turn_im_ref, shift_ref,
    pieces, tap_pieces, rows, side, filt, result, side_result, back,
    first_all, mid_all, inv_all, last_all,
    load_sem, tap_send, tap_recv, slab_send, slab_recv, in_send, in_recv, out_send, out_recv,
    side_send, side_recv, home_send, home_recv,
):
    me = lax.axis_index("seq")
    col = lax.axis_index("chan")
    count = k_ref.shape[0]
    parts = SIDE // LANES
    near = blocks // 2
    base = (me // near) * near
    local = lax.rem(me, near)
    depth = SIDE // 2
    far_first = sorted(range(1, blocks), key=lambda step: abs(step - near))

    sources = (taps_hbm, k_hbm, v_hbm, c_hbm, q_hbm, first_hbm, mid_hbm, inv_hbm, turn_re_hbm, turn_im_hbm, last_hbm, shift_hbm)
    targets = (taps_ref, k_ref, v_ref, c_ref, q_ref, first_ref, mid_ref, inv_ref, turn_re_ref, turn_im_ref, last_ref, shift_ref)
    loads = [
        pltpu.make_async_copy(source, target, load_sem.at[place])
        for place, (source, target) in enumerate(zip(sources, targets))
    ]
    for load in loads:
        load.start()

    barrier = pltpu.get_barrier_semaphore()
    for step in range(1, blocks):
        pl.semaphore_signal(barrier, inc=1, device_id=(lax.rem(me + step, blocks), col), device_id_type=MESH)
    for step in range(1, groups):
        pl.semaphore_signal(barrier, inc=1, device_id=(me, lax.rem(col + step, groups)), device_id_type=MESH)

    def span(row, part):
        return slice(row * SIDE + part * LANES, row * SIDE + (part + 1) * LANES)

    loads[0].wait()
    for part in range(parts):
        for row in range(taps_ref.shape[1] // SIDE):
            tap_pieces[:, part, row, :] = taps_ref[:, span(row, part)]
    tap_copies, slab_copies, side_copies, home_copies = [], [], [], []
    in_copies, out_copies = [[] for _ in range(parts)], [[] for _ in range(parts)]
    pl.semaphore_wait(barrier, blocks + groups - 2)
    for step in far_first:
        target = lax.rem(me + step, blocks)
        copy = pltpu.make_async_remote_copy(
            src_ref=tap_pieces.at[lax.rem(target, count)], dst_ref=filt.at[me, col],
            send_sem=tap_send.at[step], recv_sem=tap_recv.at[step],
            device_id=(target, col), device_id_type=MESH,
        )
        copy.start()
        tap_copies.append(copy)

    for load in loads[1:5]:
        load.wait()
    for part in range(parts):
        for row in range(k_ref.shape[1] // SIDE):
            tokens = span(row, part)
            pieces[:count, part, row, :] = k_ref[:, tokens] * v_ref[:, tokens]
            pieces[count:, part, row, :] = c_ref[:, tokens] * q_ref[:, tokens]
        for step in far_first[:near - 1]:
            target = lax.rem(me + step, blocks)
            copy = pltpu.make_async_remote_copy(
                src_ref=pieces.at[lax.rem(target + near, blocks), part], dst_ref=rows.at[part, me],
                send_sem=in_send.at[part, step], recv_sem=in_recv.at[part, step],
                device_id=(target, col), device_id_type=MESH,
            )
            copy.start()
            in_copies[part].append(copy)
        for step in range(1, near if part == parts - 1 else 1):
            target = base + lax.rem(me + step, near)
            copy = pltpu.make_async_remote_copy(
                src_ref=pieces.at[target], dst_ref=side.at[local],
                send_sem=side_send.at[step], recv_sem=side_recv.at[step],
                device_id=(target, col), device_id_type=MESH,
            )
            copy.start()
            side_copies.append(copy)
        for step in far_first[near - 1:]:
            target = lax.rem(me + step, blocks)
            copy = pltpu.make_async_remote_copy(
                src_ref=pieces.at[lax.rem(target + near, blocks), part], dst_ref=rows.at[part, me],
                send_sem=in_send.at[part, step], recv_sem=in_recv.at[part, step],
                device_id=(target, col), device_id_type=MESH,
            )
            copy.start()
            in_copies[part].append(copy)
    side[local] = pieces[me]
    filt[me, col] = tap_pieces[lax.rem(me, count)]
    for part in range(parts):
        rows[part, me] = pieces[lax.rem(me + near, blocks), part]

    for copy in tap_copies:
        copy.wait_recv()
    for step in range(1, groups):
        copy = pltpu.make_async_remote_copy(
            src_ref=filt.at[:, col], dst_ref=filt.at[:, col],
            send_sem=slab_send.at[step], recv_sem=slab_recv.at[step],
            device_id=(me, lax.rem(col + step, groups)), device_id_type=MESH,
        )
        copy.start()
        slab_copies.append(copy)

    for load in loads[5:]:
        load.wait()
    first_all[...] = stack_left(first_ref[...])
    last_all[...] = stack_left(last_ref[...])
    mid_all[...] = stack_right(mid_ref[...])
    inv_all[...] = stack_right(inv_ref[...])
    shift_re, shift_im = shift_ref[0:1, :], shift_ref[1:2, :]

    def twisted(mixed, part):
        cut = slice(part * LANES, (part + 1) * LANES)
        real, imag = mixed[:SIDE], mixed[SIDE:]
        turn_re, turn_im = turn_re_ref[:, cut], turn_im_ref[:, cut]
        return real * turn_re - imag * turn_im, real * turn_im + imag * turn_re

    def spectrum(near_part, far_part):
        (near_re, near_im), (far_re, far_im) = near_part, far_part
        gap_re, gap_im = near_re - far_re, near_im - far_im
        even = jnp.concatenate([near_re + far_re, near_im + far_im], axis=1)
        odd = jnp.concatenate(
            [gap_re * shift_re - gap_im * shift_im, gap_re * shift_im + gap_im * shift_re], axis=1
        )
        total = mul(stack_left(jnp.concatenate([even, odd], axis=0)), mid_all[...])
        return total[:, :LANES], total[:, LANES:]

    def levels(row_re, row_im, tap_re, tap_im):
        joined = jnp.concatenate(
            [row_re * tap_re - row_im * tap_im, row_re * tap_im + row_im * tap_re], axis=1
        )
        coarse = mul(stack_left(joined), inv_all[...])
        even_re, even_im = coarse[:SIDE, :LANES], coarse[:SIDE, LANES:]
        odd_re, odd_im = coarse[SIDE:, :LANES], coarse[SIDE:, LANES:]
        gap_re = odd_re * shift_re + odd_im * shift_im
        gap_im = odd_im * shift_re - odd_re * shift_im
        found = []
        for part, real, imag in ((0, even_re + gap_re, even_im + gap_im), (1, even_re - gap_re, even_im - gap_im)):
            cut = slice(part * LANES, (part + 1) * LANES)
            turn_re, turn_im = turn_re_ref[:, cut], turn_im_ref[:, cut]
            found.append(jnp.concatenate(
                [real * turn_re + imag * turn_im, imag * turn_re - real * turn_im], axis=0
            ))
        return found

    def row_part(part):
        for copy in in_copies[part]:
            copy.wait_recv()
        return twisted(mul(first_all[...], stack_right(rows[part].reshape(SIDE, LANES))), part)

    row_near = row_part(0)
    for copy in side_copies:
        copy.wait_recv()
    tokens = jnp.concatenate([side[:, part].reshape(depth, LANES) for part in range(parts)], axis=1)
    held = jnp.concatenate([first_all[:, third * SIDE:third * SIDE + depth] for third in range(3)], axis=1)
    mixed = mul(held, stack_right(tokens))
    side_re, side_im = spectrum(twisted(mixed[:, :LANES], 0), twisted(mixed[:, LANES:], 1))
    for copy in slab_copies:
        copy.wait_recv()
    taps = jnp.concatenate([filt[:, :, part].reshape(SIDE, LANES) for part in range(parts)], axis=1)
    mixed = mul(first_all[...], stack_right(taps))
    tap_re, tap_im = spectrum(twisted(mixed[:, :LANES], 0), twisted(mixed[:, LANES:], 1))
    tap_im = tap_im * jnp.where(me < near, -1.0, 1.0)

    level = jnp.concatenate(levels(side_re, side_im, tap_re, -tap_im), axis=1)
    rebuilt = mul(last_all[:depth], stack_right(level))
    for part in range(parts):
        side_result[:, part] = rebuilt[:, part * LANES:(part + 1) * LANES].reshape(near, *side_result.shape[2:])
    for step in range(1, near):
        target = lax.rem(me + step, near)
        copy = pltpu.make_async_remote_copy(
            src_ref=side_result.at[target], dst_ref=back.at[me],
            send_sem=home_send.at[step], recv_sem=home_recv.at[step],
            device_id=(base + target, col), device_id_type=MESH,
        )
        copy.start()
        home_copies.append(copy)
    back[me] = side_result[local]

    row_re, row_im = spectrum(row_near, row_part(1))
    kept = pl.ds(pl.multiple_of((me // near) * depth, depth), depth)
    place = lax.rem(me + near, blocks)
    for part, level in enumerate(levels(row_re, row_im, tap_re, tap_im)):
        result[part] = mul(last_all[kept, :], stack_right(level)).reshape(result.shape[1:])
        for step in range(1, near):
            target = lax.rem(me + step, near)
            copy = pltpu.make_async_remote_copy(
                src_ref=result.at[part, target], dst_ref=back.at[place, part],
                send_sem=out_send.at[part, step], recv_sem=out_recv.at[part, step],
                device_id=(base + target, col), device_id_type=MESH,
            )
            copy.start()
            out_copies[part].append(copy)
        back[place, part] = result[part, local]
    for copy in home_copies:
        copy.wait_recv()
    for part in range(parts):
        for copy in out_copies[part]:
            copy.wait_recv()
        for row in range(back.shape[2]):
            out_ref[:, span(row, part)] = back[:, part, row, :]
    for copy in tap_copies + sum(in_copies, []) + slab_copies + side_copies + home_copies + sum(out_copies, []):
        copy.wait_send()


def rows_on_device(query_gate, key_gate, value_input, filter_taps, cotangent):
    count, width = query_gate.shape
    blocks = lax.axis_size("seq")
    groups = lax.axis_size("chan")
    high = width // SIDE
    near = blocks // 2
    parts = SIDE // LANES
    tables = fourier_tables()
    f32, bf16 = jnp.float32, jnp.bfloat16
    operands = (key_gate, value_input, query_gate, cotangent, filter_taps, *[jnp.asarray(table) for table in tables])
    sums = pl.pallas_call(
        partial(row_kernel, blocks, groups),
        out_shape=jax.ShapeDtypeStruct((blocks, width), f32),
        in_specs=[pl.BlockSpec(memory_space=pl.ANY)] * len(operands),
        out_specs=pl.BlockSpec(memory_space=pltpu.VMEM),
        scratch_shapes=[
            *[pltpu.VMEM(operand.shape, f32) for operand in operands],
            pltpu.VMEM((blocks, parts, high, LANES), f32),
            pltpu.VMEM((count, parts, high // groups, LANES), f32),
            pltpu.VMEM((parts, blocks, high, LANES), f32),
            pltpu.VMEM((near, parts, high, LANES), f32),
            pltpu.VMEM((blocks, groups, parts, high // groups, LANES), f32),
            pltpu.VMEM((parts, near, high, LANES), f32),
            pltpu.VMEM((near, parts, high, LANES), f32),
            pltpu.VMEM((blocks, parts, high, LANES), f32),
            pltpu.VMEM((2 * SIDE, 3 * SIDE), bf16),
            pltpu.VMEM((3 * SIDE, SIDE), bf16),
            pltpu.VMEM((3 * SIDE, SIDE), bf16),
            pltpu.VMEM((SIDE, 6 * SIDE), bf16),
            pltpu.SemaphoreType.DMA((len(operands),)),
            pltpu.SemaphoreType.DMA((blocks,)),
            pltpu.SemaphoreType.DMA((blocks,)),
            pltpu.SemaphoreType.DMA((groups,)),
            pltpu.SemaphoreType.DMA((groups,)),
            pltpu.SemaphoreType.DMA((parts, blocks)),
            pltpu.SemaphoreType.DMA((parts, blocks)),
            pltpu.SemaphoreType.DMA((parts, blocks)),
            pltpu.SemaphoreType.DMA((parts, blocks)),
            *[pltpu.SemaphoreType.DMA((near,))] * 4,
        ],
        compiler_params=pltpu.CompilerParams(
            collective_id=0, has_side_effects=True, vmem_limit_bytes=VMEM_BYTES
        ),
    )(*operands)
    convolved, gated_grad = sums[:count], sums[count:]
    return (cotangent * convolved, gated_grad * value_input, gated_grad * key_gate)


def one_row_each(query_gate, filter_taps):
    count, width = query_gate.shape
    blocks = lax.axis_size("seq")
    groups = lax.axis_size("chan")
    return (
        blocks == 2 * count
        and filter_taps.shape[0] == count
        and blocks * width == SIDE * SIDE
        and width % (8 * groups * SIDE) == 0
    )


def phase_table(row_count, column_count, offset, period, direction):
    row_index = lax.broadcasted_iota(jnp.int32, (row_count, column_count), 0)
    column_index = lax.broadcasted_iota(jnp.int32, (row_count, column_count), 1)
    phases = row_index * (column_index + offset) % period
    angles = phases.astype(jnp.float32) * (direction * 2.0 * math.pi / period)
    return (jnp.cos(angles), jnp.sin(angles))


def complex_mix(formula, table_real, table_imag, data_real, data_imag):
    product = partial(jnp.einsum, formula, precision=lax.Precision.HIGHEST)
    return (
        product(table_real, data_real) - product(table_imag, data_imag),
        product(table_real, data_imag) + product(table_imag, data_real),
    )


def regroup_tokens(signal):
    return lax.all_to_all(signal, "seq", split_axis=1, concat_axis=1, tiled=True)


def regroup_spectrum(part_real, part_imag):
    return (
        lax.all_to_all(part_real, "seq", split_axis=1, concat_axis=1, tiled=True),
        lax.all_to_all(part_imag, "seq", split_axis=1, concat_axis=1, tiled=True),
    )


def finish_forward(moved_real, moved_imag, blocks, width, tokens):
    outer_real, outer_imag = phase_table(blocks, blocks, 0, blocks, -1.0)
    coarse_real, coarse_imag = complex_mix(
        "ur,crjq->cujq", outer_real, outer_imag, moved_real, moved_imag
    )
    shift_real, shift_imag = phase_table(blocks, width, 0, tokens, -1.0)
    shift_real = shift_real[None, :, None, :]
    shift_imag = shift_imag[None, :, None, :]
    twisted_real = coarse_real * shift_real - coarse_imag * shift_imag
    twisted_imag = coarse_real * shift_imag + coarse_imag * shift_real
    inner_real, inner_imag = phase_table(width, width, 0, width, -1.0)
    return complex_mix("qv,cujq->cujv", inner_real, inner_imag, twisted_real, twisted_imag)


def start_inverse(spectrum_real, spectrum_imag, blocks, width, tokens):
    inner_real, inner_imag = phase_table(width, width, 0, width, 1.0)
    fine_real, fine_imag = complex_mix(
        "vq,cujv->cujq", inner_real, inner_imag, spectrum_real, spectrum_imag
    )
    shift_real, shift_imag = phase_table(blocks, width, 0, tokens, 1.0)
    shift_real = shift_real[None, :, None, :]
    shift_imag = shift_imag[None, :, None, :]
    untwisted_real = fine_real * shift_real - fine_imag * shift_imag
    untwisted_imag = fine_real * shift_imag + fine_imag * shift_real
    outer_real, outer_imag = phase_table(blocks, blocks, 0, blocks, 1.0)
    return complex_mix("ru,cujq->crjq", outer_real, outer_imag, untwisted_real, untwisted_imag)


def forward_spectrum(signal):
    count, tokens = signal.shape
    blocks = lax.axis_size("seq")
    width = tokens // blocks
    freqs = 2 * blocks
    period = freqs * tokens
    rank = lax.axis_index("seq")
    gathered = regroup_tokens(signal.reshape(count, blocks, width))
    product = partial(jnp.einsum, "kp,cpq->ckq", precision=lax.Precision.HIGHEST)
    anchor = rank * width
    first_real, first_imag = phase_table(freqs, blocks, 0, freqs, -1.0)
    mixed_real = product(first_real, gathered)
    mixed_imag = product(first_imag, gathered)
    turn_real, turn_imag = phase_table(freqs, width, anchor, period, -1.0)
    moved_real, moved_imag = regroup_spectrum(
        mixed_real * turn_real - mixed_imag * turn_imag,
        mixed_real * turn_imag + mixed_imag * turn_real,
    )
    moved_real = moved_real.reshape(count, blocks, 2, width)
    moved_imag = moved_imag.reshape(count, blocks, 2, width)
    return finish_forward(moved_real, moved_imag, blocks, width, tokens)


def inverse_spectrum(spectrum_real, spectrum_imag):
    count, blocks, per_device, width = spectrum_real.shape
    tokens = blocks * width
    freqs = 2 * blocks
    period = freqs * tokens
    rank = lax.axis_index("seq")
    spread_real, spread_imag = start_inverse(spectrum_real, spectrum_imag, blocks, width, tokens)
    product = partial(jnp.einsum, "kp,ckq->cpq", precision=lax.Precision.HIGHEST)
    anchor = rank * width
    moved_real, moved_imag = regroup_spectrum(
        spread_real.reshape(count, blocks * per_device, width),
        spread_imag.reshape(count, blocks * per_device, width),
    )
    turn_real, turn_imag = phase_table(freqs, width, anchor, period, 1.0)
    level_real = moved_real * turn_real - moved_imag * turn_imag
    level_imag = moved_real * turn_imag + moved_imag * turn_real
    first_real, first_imag = phase_table(freqs, blocks, 0, freqs, 1.0)
    rebuilt = (product(first_real, level_real) - product(first_imag, level_imag)) * (1.0 / period)
    return regroup_tokens(rebuilt).reshape(count, tokens)


def on_device(query_gate, key_gate, value_input, filter_taps, cotangent):
    if one_row_each(query_gate, filter_taps):
        return rows_on_device(query_gate, key_gate, value_input, filter_taps, cotangent)
    block_taps = lax.all_gather(filter_taps, "chan", axis=1, tiled=True)
    filter_real, filter_imag = forward_spectrum(block_taps)
    gated = key_gate * value_input
    weighted = cotangent * query_gate
    gated_real, gated_imag = forward_spectrum(gated)
    convolved = inverse_spectrum(
        gated_real * filter_real - gated_imag * filter_imag,
        gated_real * filter_imag + gated_imag * filter_real,
    )
    weighted_real, weighted_imag = forward_spectrum(weighted)
    gated_grad = inverse_spectrum(
        weighted_real * filter_real + weighted_imag * filter_imag,
        weighted_imag * filter_real - weighted_real * filter_imag,
    )
    return (cotangent * convolved, gated_grad * value_input, gated_grad * key_gate)


def solution(mesh):
    in_specs = (
        P("chan", "seq"),
        P("chan", "seq"),
        P("chan", "seq"),
        P(None, ("seq", "chan")),
        P("chan", "seq"),
    )
    out_specs = (P("chan", "seq"), P("chan", "seq"), P("chan", "seq"))
    return jax.shard_map(
        on_device, mesh=mesh, in_specs=in_specs, out_specs=out_specs, check_vma=False
    )
```

```python
from functools import partial
import math

import jax
import jax.numpy as jnp
import numpy as np
from jax import lax
from jax.experimental import pallas as pl
from jax.experimental.pallas import tpu as pltpu
from jax.sharding import PartitionSpec as P

MESH = pl.DeviceIdType.MESH
SIDE = 256
LANES = 128
VMEM_BYTES = 63 * 1024 * 1024


def fourier_tables():
    total = SIDE * SIDE
    index = np.arange(SIDE, dtype=np.float64)
    outer = 2.0 * np.pi * np.outer(index + 0.25, index) / SIDE
    first = np.concatenate([np.cos(outer), -np.sin(outer)], axis=0)
    last = first.T / total
    inner_index = np.arange(LANES, dtype=np.float64)
    inner = 2.0 * np.pi * (np.outer(inner_index, inner_index) % LANES) / LANES
    cosine, sine = np.cos(inner), np.sin(inner)
    middle = np.block([[cosine, -sine], [sine, cosine]])
    inverse = np.block([[cosine, sine], [-sine, cosine]])
    twist = 2.0 * np.pi * np.outer(index + 0.25, index) / total
    odd = 2.0 * np.pi * inner_index / SIDE
    shift = np.stack([np.cos(odd), -np.sin(odd)] * 4)
    tables = (first, middle, inverse, last, np.cos(twist), -np.sin(twist), shift)
    return tuple(table.astype(np.float32) for table in tables)


def split(value):
    high = value.astype(jnp.bfloat16)
    low = (value - high.astype(jnp.float32)).astype(jnp.bfloat16)
    return high, low


def stack_left(value, axis=1):
    high, low = split(value)
    return jnp.concatenate([high, high, low], axis=axis)


def stack_right(value, axis=0):
    high, low = split(value)
    return jnp.concatenate([high, low, high], axis=axis)


def mul(left, right):
    return jnp.dot(left, right, preferred_element_type=jnp.float32)


def row_kernel(
    blocks, groups, k_hbm, v_hbm, q_hbm, c_hbm, taps_hbm,
    first_hbm, mid_hbm, inv_hbm, last_hbm, turn_re_hbm, turn_im_hbm, shift_hbm, out_ref,
    k_ref, v_ref, q_ref, c_ref, taps_ref, first_ref, mid_ref, inv_ref, last_ref, turn_re_ref, turn_im_ref, shift_ref,
    pieces, tap_pieces, rows, side, filt, result, side_result, back,
    first_all, mid_all, inv_all, last_all, staged, store_sem,
    load_sem, tap_send, tap_recv, slab_send, slab_recv, in_send, in_recv, out_send, out_recv,
    side_send, side_recv, home_send, home_recv,
):
    me = lax.axis_index("seq")
    col = lax.axis_index("chan")
    count = k_ref.shape[0]
    parts = SIDE // LANES
    near = blocks // 2
    base = (me // near) * near
    local = lax.rem(me, near)
    depth = SIDE // 2

    sources = (taps_hbm, k_hbm, v_hbm, c_hbm, q_hbm, first_hbm, mid_hbm, inv_hbm, turn_re_hbm, turn_im_hbm, last_hbm, shift_hbm)
    targets = (taps_ref, k_ref, v_ref, c_ref, q_ref, first_ref, mid_ref, inv_ref, turn_re_ref, turn_im_ref, last_ref, shift_ref)
    loads = [
        pltpu.make_async_copy(source, target, load_sem.at[place])
        for place, (source, target) in enumerate(zip(sources, targets))
    ]
    for load in loads:
        load.start()

    barrier = pltpu.get_barrier_semaphore()
    for step in range(1, blocks):
        pl.semaphore_signal(barrier, inc=1, device_id=(lax.rem(me + step, blocks), col), device_id_type=MESH)
    for step in range(1, groups):
        pl.semaphore_signal(barrier, inc=1, device_id=(me, lax.rem(col + step, groups)), device_id_type=MESH)

    def span(row, part):
        return slice(row * SIDE + part * LANES, row * SIDE + (part + 1) * LANES)

    loads[0].wait()
    for part in range(parts):
        for row in range(taps_ref.shape[1] // SIDE):
            tap_pieces[:, part, row, :] = taps_ref[:, span(row, part)]
    tap_copies, slab_copies, side_copies, home_copies = [], [], [], []
    in_copies, out_copies = [[] for _ in range(parts)], [[] for _ in range(parts)]
    pl.semaphore_wait(barrier, blocks + groups - 2)
    for step in range(1, blocks):
        target = lax.rem(me + step, blocks)
        copy = pltpu.make_async_remote_copy(
            src_ref=tap_pieces.at[lax.rem(target, count)], dst_ref=filt.at[me, col],
            send_sem=tap_send.at[step], recv_sem=tap_recv.at[step],
            device_id=(target, col), device_id_type=MESH,
        )
        copy.start()
        tap_copies.append(copy)

    for load in loads[1:5]:
        load.wait()
    for part in range(parts):
        for row in range(k_ref.shape[1] // SIDE):
            tokens = span(row, part)
            pieces[:count, part, row, :] = k_ref[:, tokens] * v_ref[:, tokens]
            pieces[count:, part, row, :] = c_ref[:, tokens] * q_ref[:, tokens]
        for step in range(1, near if part == parts - 1 else 1):
            target = base + lax.rem(me + step, near)
            copy = pltpu.make_async_remote_copy(
                src_ref=pieces.at[target], dst_ref=side.at[local],
                send_sem=side_send.at[step], recv_sem=side_recv.at[step],
                device_id=(target, col), device_id_type=MESH,
            )
            copy.start()
            side_copies.append(copy)
        for step in range(1, blocks):
            target = lax.rem(me + step, blocks)
            copy = pltpu.make_async_remote_copy(
                src_ref=pieces.at[lax.rem(target + near, blocks), part], dst_ref=rows.at[part, me],
                send_sem=in_send.at[part, step], recv_sem=in_recv.at[part, step],
                device_id=(target, col), device_id_type=MESH,
            )
            copy.start()
            in_copies[part].append(copy)
    side[local] = pieces[me]
    filt[me, col] = tap_pieces[lax.rem(me, count)]
    for part in range(parts):
        rows[part, me] = pieces[lax.rem(me + near, blocks), part]

    for copy in tap_copies:
        copy.wait_recv()
    for step in range(1, groups):
        copy = pltpu.make_async_remote_copy(
            src_ref=filt.at[:, col], dst_ref=filt.at[:, col],
            send_sem=slab_send.at[step], recv_sem=slab_recv.at[step],
            device_id=(me, lax.rem(col + step, groups)), device_id_type=MESH,
        )
        copy.start()
        slab_copies.append(copy)

    for load in loads[5:]:
        load.wait()
    first_all[...] = stack_left(first_ref[...])
    last_all[...] = stack_left(last_ref[...])
    mid_all[...] = stack_right(mid_ref[...])
    inv_all[...] = stack_right(inv_ref[...])
    shift_re, shift_im = shift_ref[0:1, :], shift_ref[1:2, :]

    def twisted(mixed, part):
        cut = slice(part * LANES, (part + 1) * LANES)
        real, imag = mixed[:SIDE], mixed[SIDE:]
        turn_re, turn_im = turn_re_ref[:, cut], turn_im_ref[:, cut]
        return real * turn_re - imag * turn_im, real * turn_im + imag * turn_re

    def spectrum(near_part, far_part):
        (near_re, near_im), (far_re, far_im) = near_part, far_part
        gap_re, gap_im = near_re - far_re, near_im - far_im
        even = jnp.concatenate([near_re + far_re, near_im + far_im], axis=1)
        odd = jnp.concatenate(
            [gap_re * shift_re - gap_im * shift_im, gap_re * shift_im + gap_im * shift_re], axis=1
        )
        total = mul(stack_left(jnp.concatenate([even, odd], axis=0)), mid_all[...])
        return total[:, :LANES], total[:, LANES:]

    def levels(row_re, row_im, tap_re, tap_im):
        joined = jnp.concatenate(
            [row_re * tap_re - row_im * tap_im, row_re * tap_im + row_im * tap_re], axis=1
        )
        coarse = mul(stack_left(joined), inv_all[...])
        even_re, even_im = coarse[:SIDE, :LANES], coarse[:SIDE, LANES:]
        odd_re, odd_im = coarse[SIDE:, :LANES], coarse[SIDE:, LANES:]
        gap_re = odd_re * shift_re + odd_im * shift_im
        gap_im = odd_im * shift_re - odd_re * shift_im
        found = []
        for part, real, imag in ((0, even_re + gap_re, even_im + gap_im), (1, even_re - gap_re, even_im - gap_im)):
            cut = slice(part * LANES, (part + 1) * LANES)
            turn_re, turn_im = turn_re_ref[:, cut], turn_im_ref[:, cut]
            found.append(jnp.concatenate(
                [real * turn_re + imag * turn_im, imag * turn_re - real * turn_im], axis=0
            ))
        return found

    def row_part(part):
        for copy in in_copies[part]:
            copy.wait_recv()
        return twisted(mul(first_all[...], stack_right(rows[part].reshape(SIDE, LANES))), part)

    row_near = row_part(0)
    for copy in side_copies:
        copy.wait_recv()
    tokens = jnp.concatenate([side[:, part].reshape(depth, LANES) for part in range(parts)], axis=1)
    held = jnp.concatenate([first_all[:, third * SIDE:third * SIDE + depth] for third in range(3)], axis=1)
    mixed = mul(held, stack_right(tokens))
    side_re, side_im = spectrum(twisted(mixed[:, :LANES], 0), twisted(mixed[:, LANES:], 1))
    for copy in slab_copies:
        copy.wait_recv()
    taps = jnp.concatenate([filt[:, :, part].reshape(SIDE, LANES) for part in range(parts)], axis=1)
    mixed = mul(first_all[...], stack_right(taps))
    tap_re, tap_im = spectrum(twisted(mixed[:, :LANES], 0), twisted(mixed[:, LANES:], 1))
    tap_im = tap_im * jnp.where(me < near, -1.0, 1.0)

    level = jnp.concatenate(levels(side_re, side_im, tap_re, -tap_im), axis=1)
    rebuilt = mul(last_all[:depth], stack_right(level))
    for part in range(parts):
        side_result[:, part] = rebuilt[:, part * LANES:(part + 1) * LANES].reshape(near, *side_result.shape[2:])
    for step in range(1, near):
        target = lax.rem(me + step, near)
        copy = pltpu.make_async_remote_copy(
            src_ref=side_result.at[target], dst_ref=back.at[me],
            send_sem=home_send.at[step], recv_sem=home_recv.at[step],
            device_id=(base + target, col), device_id_type=MESH,
        )
        copy.start()
        home_copies.append(copy)
    back[me] = side_result[local]

    row_re, row_im = spectrum(row_near, row_part(1))
    kept = pl.ds(pl.multiple_of((me // near) * depth, depth), depth)
    place = lax.rem(me + near, blocks)
    for part, level in enumerate(levels(row_re, row_im, tap_re, tap_im)):
        result[part] = mul(last_all[kept, :], stack_right(level)).reshape(result.shape[1:])
        for step in range(1, near):
            target = lax.rem(me + step, near)
            copy = pltpu.make_async_remote_copy(
                src_ref=result.at[part, target], dst_ref=back.at[place, part],
                send_sem=out_send.at[part, step], recv_sem=out_recv.at[part, step],
                device_id=(base + target, col), device_id_type=MESH,
            )
            copy.start()
            out_copies[part].append(copy)
        back[place, part] = result[part, local]
    half = me // near
    for copy in home_copies:
        copy.wait_recv()
    for part in range(parts):
        for row in range(back.shape[2]):
            staged[half, :, span(row, part)] = back[pl.ds(half * count, count), part, row, :]
    side_store = pltpu.make_async_copy(staged.at[half], out_ref.at[half], store_sem.at[0])
    side_store.start()
    for part in range(parts):
        for copy in out_copies[part]:
            copy.wait_recv()
        for row in range(back.shape[2]):
            staged[1 - half, :, span(row, part)] = back[pl.ds((1 - half) * count, count), part, row, :]
    main_store = pltpu.make_async_copy(staged.at[1 - half], out_ref.at[1 - half], store_sem.at[1])
    main_store.start()
    side_store.wait()
    main_store.wait()
    for copy in tap_copies + sum(in_copies, []) + slab_copies + side_copies + home_copies + sum(out_copies, []):
        copy.wait_send()


def rows_on_device(query_gate, key_gate, value_input, filter_taps, cotangent):
    count, width = query_gate.shape
    blocks = lax.axis_size("seq")
    groups = lax.axis_size("chan")
    high = width // SIDE
    near = blocks // 2
    parts = SIDE // LANES
    tables = fourier_tables()
    f32, bf16 = jnp.float32, jnp.bfloat16
    operands = (key_gate, value_input, query_gate, cotangent, filter_taps, *[jnp.asarray(table) for table in tables])
    sums = pl.pallas_call(
        partial(row_kernel, blocks, groups),
        out_shape=jax.ShapeDtypeStruct((2, count, width), f32),
        in_specs=[pl.BlockSpec(memory_space=pl.ANY)] * len(operands),
        out_specs=pl.BlockSpec(memory_space=pl.ANY),
        scratch_shapes=[
            *[pltpu.VMEM(operand.shape, f32) for operand in operands],
            pltpu.VMEM((blocks, parts, high, LANES), f32),
            pltpu.VMEM((count, parts, high // groups, LANES), f32),
            pltpu.VMEM((parts, blocks, high, LANES), f32),
            pltpu.VMEM((near, parts, high, LANES), f32),
            pltpu.VMEM((blocks, groups, parts, high // groups, LANES), f32),
            pltpu.VMEM((parts, near, high, LANES), f32),
            pltpu.VMEM((near, parts, high, LANES), f32),
            pltpu.VMEM((blocks, parts, high, LANES), f32),
            pltpu.VMEM((2 * SIDE, 3 * SIDE), bf16),
            pltpu.VMEM((3 * SIDE, SIDE), bf16),
            pltpu.VMEM((3 * SIDE, SIDE), bf16),
            pltpu.VMEM((SIDE, 6 * SIDE), bf16),
            pltpu.VMEM((2, count, width), f32),
            pltpu.SemaphoreType.DMA((2,)),
            pltpu.SemaphoreType.DMA((len(operands),)),
            pltpu.SemaphoreType.DMA((blocks,)),
            pltpu.SemaphoreType.DMA((blocks,)),
            pltpu.SemaphoreType.DMA((groups,)),
            pltpu.SemaphoreType.DMA((groups,)),
            pltpu.SemaphoreType.DMA((parts, blocks)),
            pltpu.SemaphoreType.DMA((parts, blocks)),
            pltpu.SemaphoreType.DMA((parts, blocks)),
            pltpu.SemaphoreType.DMA((parts, blocks)),
            *[pltpu.SemaphoreType.DMA((near,))] * 4,
        ],
        compiler_params=pltpu.CompilerParams(
            collective_id=0, has_side_effects=True, vmem_limit_bytes=VMEM_BYTES
        ),
    )(*operands)
    convolved, gated_grad = sums[0], sums[1]
    return (cotangent * convolved, gated_grad * value_input, gated_grad * key_gate)


def one_row_each(query_gate, filter_taps):
    count, width = query_gate.shape
    blocks = lax.axis_size("seq")
    groups = lax.axis_size("chan")
    return (
        blocks == 2 * count
        and filter_taps.shape[0] == count
        and blocks * width == SIDE * SIDE
        and width % (8 * groups * SIDE) == 0
    )


def phase_table(row_count, column_count, offset, period, direction):
    row_index = lax.broadcasted_iota(jnp.int32, (row_count, column_count), 0)
    column_index = lax.broadcasted_iota(jnp.int32, (row_count, column_count), 1)
    phases = row_index * (column_index + offset) % period
    angles = phases.astype(jnp.float32) * (direction * 2.0 * math.pi / period)
    return (jnp.cos(angles), jnp.sin(angles))


def complex_mix(formula, table_real, table_imag, data_real, data_imag):
    product = partial(jnp.einsum, formula, precision=lax.Precision.HIGHEST)
    return (
        product(table_real, data_real) - product(table_imag, data_imag),
        product(table_real, data_imag) + product(table_imag, data_real),
    )


def regroup_tokens(signal):
    return lax.all_to_all(signal, "seq", split_axis=1, concat_axis=1, tiled=True)


def regroup_spectrum(part_real, part_imag):
    return (
        lax.all_to_all(part_real, "seq", split_axis=1, concat_axis=1, tiled=True),
        lax.all_to_all(part_imag, "seq", split_axis=1, concat_axis=1, tiled=True),
    )


def finish_forward(moved_real, moved_imag, blocks, width, tokens):
    outer_real, outer_imag = phase_table(blocks, blocks, 0, blocks, -1.0)
    coarse_real, coarse_imag = complex_mix(
        "ur,crjq->cujq", outer_real, outer_imag, moved_real, moved_imag
    )
    shift_real, shift_imag = phase_table(blocks, width, 0, tokens, -1.0)
    shift_real = shift_real[None, :, None, :]
    shift_imag = shift_imag[None, :, None, :]
    twisted_real = coarse_real * shift_real - coarse_imag * shift_imag
    twisted_imag = coarse_real * shift_imag + coarse_imag * shift_real
    inner_real, inner_imag = phase_table(width, width, 0, width, -1.0)
    return complex_mix("qv,cujq->cujv", inner_real, inner_imag, twisted_real, twisted_imag)


def start_inverse(spectrum_real, spectrum_imag, blocks, width, tokens):
    inner_real, inner_imag = phase_table(width, width, 0, width, 1.0)
    fine_real, fine_imag = complex_mix(
        "vq,cujv->cujq", inner_real, inner_imag, spectrum_real, spectrum_imag
    )
    shift_real, shift_imag = phase_table(blocks, width, 0, tokens, 1.0)
    shift_real = shift_real[None, :, None, :]
    shift_imag = shift_imag[None, :, None, :]
    untwisted_real = fine_real * shift_real - fine_imag * shift_imag
    untwisted_imag = fine_real * shift_imag + fine_imag * shift_real
    outer_real, outer_imag = phase_table(blocks, blocks, 0, blocks, 1.0)
    return complex_mix("ru,cujq->crjq", outer_real, outer_imag, untwisted_real, untwisted_imag)


def forward_spectrum(signal):
    count, tokens = signal.shape
    blocks = lax.axis_size("seq")
    width = tokens // blocks
    freqs = 2 * blocks
    period = freqs * tokens
    rank = lax.axis_index("seq")
    gathered = regroup_tokens(signal.reshape(count, blocks, width))
    product = partial(jnp.einsum, "kp,cpq->ckq", precision=lax.Precision.HIGHEST)
    anchor = rank * width
    first_real, first_imag = phase_table(freqs, blocks, 0, freqs, -1.0)
    mixed_real = product(first_real, gathered)
    mixed_imag = product(first_imag, gathered)
    turn_real, turn_imag = phase_table(freqs, width, anchor, period, -1.0)
    moved_real, moved_imag = regroup_spectrum(
        mixed_real * turn_real - mixed_imag * turn_imag,
        mixed_real * turn_imag + mixed_imag * turn_real,
    )
    moved_real = moved_real.reshape(count, blocks, 2, width)
    moved_imag = moved_imag.reshape(count, blocks, 2, width)
    return finish_forward(moved_real, moved_imag, blocks, width, tokens)


def inverse_spectrum(spectrum_real, spectrum_imag):
    count, blocks, per_device, width = spectrum_real.shape
    tokens = blocks * width
    freqs = 2 * blocks
    period = freqs * tokens
    rank = lax.axis_index("seq")
    spread_real, spread_imag = start_inverse(spectrum_real, spectrum_imag, blocks, width, tokens)
    product = partial(jnp.einsum, "kp,ckq->cpq", precision=lax.Precision.HIGHEST)
    anchor = rank * width
    moved_real, moved_imag = regroup_spectrum(
        spread_real.reshape(count, blocks * per_device, width),
        spread_imag.reshape(count, blocks * per_device, width),
    )
    turn_real, turn_imag = phase_table(freqs, width, anchor, period, 1.0)
    level_real = moved_real * turn_real - moved_imag * turn_imag
    level_imag = moved_real * turn_imag + moved_imag * turn_real
    first_real, first_imag = phase_table(freqs, blocks, 0, freqs, 1.0)
    rebuilt = (product(first_real, level_real) - product(first_imag, level_imag)) * (1.0 / period)
    return regroup_tokens(rebuilt).reshape(count, tokens)


def on_device(query_gate, key_gate, value_input, filter_taps, cotangent):
    if one_row_each(query_gate, filter_taps):
        return rows_on_device(query_gate, key_gate, value_input, filter_taps, cotangent)
    block_taps = lax.all_gather(filter_taps, "chan", axis=1, tiled=True)
    filter_real, filter_imag = forward_spectrum(block_taps)
    gated = key_gate * value_input
    weighted = cotangent * query_gate
    gated_real, gated_imag = forward_spectrum(gated)
    convolved = inverse_spectrum(
        gated_real * filter_real - gated_imag * filter_imag,
        gated_real * filter_imag + gated_imag * filter_real,
    )
    weighted_real, weighted_imag = forward_spectrum(weighted)
    gated_grad = inverse_spectrum(
        weighted_real * filter_real + weighted_imag * filter_imag,
        weighted_imag * filter_real - weighted_real * filter_imag,
    )
    return (cotangent * convolved, gated_grad * value_input, gated_grad * key_gate)


def solution(mesh):
    in_specs = (
        P("chan", "seq"),
        P("chan", "seq"),
        P("chan", "seq"),
        P(None, ("seq", "chan")),
        P("chan", "seq"),
    )
    out_specs = (P("chan", "seq"), P("chan", "seq"), P("chan", "seq"))
    return jax.shard_map(
        on_device, mesh=mesh, in_specs=in_specs, out_specs=out_specs, check_vma=False
    )
```
